128 devices in a mesh: ta: 32 (over y, x, core), gx: 4 (over z).
Axes of the slice: x: 4, y: 4, z: 4, core: 2. Of those that a mesh axis runs over, the one named last changes fastest.
Arguments:
- field: float32 [2, 512, 8, 16384], P(None, 'gx', None, 'ta'), may hold values from -6 to 6
- ion_rate: float32 [512, 8], P('gx'), may hold values from 3.0517578e-05 to 0.00048828125
- diffraction: float32 [16384], replicated, may hold values from 0.02 to 0.2
- coupling: float32 [16384], replicated, may hold values from 0.1 to 1
Outputs:
- spectrum: float32 [2, 512, 8, 16384], P(None, ('gx', 'ta'))
The draws below stay inside these ranges and needn't reach their ends.
All inputs are finite; a program needn't handle non-finite values.
Results may differ from the reference program's by a relative error of at most 0.00017.
Values sent between devices are 32-bit elements; how exact they have to be, the bound alone decides.
A program may use at most 128 MiB of HBM per device.

```python
import math
import jax
import jax.numpy as jnp
from jax import lax

NT = 16384
XD = 128
Y = 8
NX = 512
N_GX = 4


def levels(key, dims, shards, least, largest):
    factor_of, own = 1.0, jax.random.fold_in(key, 6)
    for dim, blocks in shards:
        steps = jnp.exp(jax.random.uniform(jax.random.fold_in(own, dim), (blocks,), jnp.float32, least / len(shards), largest / len(shards)))
        factor_of = factor_of * jnp.repeat(steps, dims[dim] // blocks).reshape([-1 if axis == dim else 1 for axis in range(len(dims))])
    return factor_of


def gaussian(key, extent, spread, reach, cuts=(), dtype=jnp.bfloat16):
    gain = levels(key, extent, cuts, -0.22, 0.18) if cuts else 1.0
    values = jax.random.normal(key, extent, jnp.float32) * spread * gain
    return jnp.minimum(jnp.maximum(values, -reach), reach).astype(dtype)


def setup_inputs(seed: int = 0) -> dict:
    splits = jax.random.split(jax.random.key(seed), 5)
    field = gaussian(splits[0], (2, NX, Y, NT), 1.0, 6.0, ((1, 4), (3, 32)), jnp.float32)
    ion_rate = jnp.clip(jnp.exp(math.log(0.00048828125) - 2.7725887 * jax.random.uniform(splits[1], (NX, Y), jnp.float32) ** levels(splits[1], (NX, Y), ((0, 4),), -0.2, 0.2)), 3.0517578125e-05, 0.00048828125)
    diffraction = jnp.clip(jnp.exp(jax.random.uniform(splits[2], (NT,), jnp.float32, math.log(0.02), math.log(0.2))), 0.02, 0.2)
    coupling = jnp.clip(jnp.exp(jax.random.uniform(splits[3], (NT,), jnp.float32, math.log(0.1), math.log(1.0))), 0.1, 1.0)
    return {"field": field, "ion_rate": ion_rate, "diffraction": diffraction, "coupling": coupling}


BARRIER = 2.0
KERR = 0.5

def second_diff(padded, axis, count):

    def window(offset):
        return lax.slice_in_dim(padded, offset, offset + count, axis=axis)
    return (-window(0) + 16.0 * window(1) - 30.0 * window(2) + 16.0 * window(3) - window(4)) / 12.0

def reference(field, ion_rate, diffraction, coupling):
    padded_x = jnp.pad(field, ((0, 0), (2, 2), (0, 0), (0, 0)))
    scale = 1.0 / math.sqrt(NT)

    def one_block(start):
        part = lax.dynamic_slice_in_dim(padded_x, start, XD + 4, 1)
        centre = part[:, 2:-2]
        padded_y = jnp.pad(centre, ((0, 0), (0, 0), (2, 2), (0, 0)))
        lap = second_diff(part, 1, XD) + second_diff(padded_y, 2, Y)
        rates = lax.dynamic_slice_in_dim(ion_rate, start, XD, 0)
        real_part = centre[0]
        imag_part = centre[1]
        intensity = real_part * real_part + imag_part * imag_part
        rate = rates[:, :, None] * jnp.exp(-BARRIER / jnp.sqrt(intensity + 1.0))
        integral = jnp.cumsum(rate, axis=-1)
        plasma = 1.0 - jnp.exp(-integral)
        nonlin_re = -KERR * intensity * imag_part - plasma * real_part
        nonlin_im = KERR * intensity * real_part - plasma * imag_part
        spec_field = jnp.fft.fft(real_part + 1j * imag_part, axis=-1)
        spec_lap = jnp.fft.fft(lap[0] + 1j * lap[1], axis=-1)
        spec_nonlin = jnp.fft.fft(nonlin_re + 1j * nonlin_im, axis=-1)
        out_re = (spec_field.real - diffraction * spec_lap.imag - coupling * spec_nonlin.imag) * scale
        out_im = (spec_field.imag + diffraction * spec_lap.real + coupling * spec_nonlin.real) * scale
        return jnp.stack([out_re, out_im])
    starts = (jnp.arange(N_GX) * XD).astype(jnp.int32)
    blocks = lax.map(one_block, starts)
    return jnp.concatenate([blocks[index] for index in range(N_GX)], axis=1)
```

```python
import math

import jax
import jax.numpy as jnp
import ml_dtypes
import numpy as np
from jax import lax
from jax.experimental import pallas as pl
from jax.experimental.pallas import tpu as pltpu
from jax.sharding import PartitionSpec as P

BARRIER = 2.0
KERR = 0.5
MESH = pl.DeviceIdType.MESH
R = 128
TA = 32
GX = 4
ROWS = 4
Y = 8
F32 = jnp.float32
BF16 = jnp.bfloat16


def tables():
    index = np.arange(R)
    angle = 2.0 * np.pi / R * (np.outer(index, index) % R)
    cos, sin = np.cos(angle), np.sin(angle)
    full = np.block([[cos, sin], [-sin, cos]]).astype(np.float32)
    high = full.astype(ml_dtypes.bfloat16)
    low = (full - high.astype(np.float32)).astype(ml_dtypes.bfloat16)
    dft = np.concatenate([high, low, high], axis=1)
    turn = 2.0 * np.pi / (R * R) * np.outer(index, index)
    twist = np.stack([np.cos(turn), -np.sin(turn)]) / R
    upper = (index[:, None] <= index[None, :]).astype(np.float32)
    within = np.concatenate([upper, np.ones((R, R), np.float32)], axis=1)
    within = np.concatenate([within, within], axis=0)
    lower = (index[:, None] > index[None, :]).astype(np.float32)
    before = np.concatenate([lower, lower], axis=1)
    return (
        dft,
        twist.astype(np.float32),
        within.astype(ml_dtypes.bfloat16),
        before.astype(ml_dtypes.bfloat16),
    )


def halves(v):
    high = v.astype(BF16)
    return high, (v - high.astype(F32)).astype(BF16)


def dot(a, b):
    return jnp.dot(a, b, preferred_element_type=F32)


def dot_nt(a, b):
    return lax.dot_general(a, b, (((1,), (1,)), ((), ())), preferred_element_type=F32)


def kernel(
    ion_ref, field, coupling_in, diffraction_in, dft_in, twist_in, within_in, before_in,
    out,
    rx, fe, part, result, coupling, diffraction, dft, twist, within, before,
    const_sem, send_sem, recv_sem, halo_send, halo_recv, out_sem,
):
    me = lax.axis_index("ta")
    g = lax.axis_index("gx")
    odd = lax.rem(me, 2)
    has_left = jnp.logical_or(me > 0, g > 0)
    has_right = jnp.logical_or(me < TA - 1, g < GX - 1)
    left_ta = lax.rem(me + TA - 1, TA)
    left_gx = lax.rem(jnp.where(me == 0, g + GX - 1, g), GX)
    right_ta = lax.rem(me + 1, TA)
    right_gx = lax.rem(jnp.where(me == TA - 1, g + 1, g), GX)

    def row_at(step, parity):
        return jnp.where(parity == 0, step, ROWS - 1 - step)

    gate = pltpu.get_barrier_semaphore()

    def greet(off, carry):
        pl.semaphore_signal(
            gate, inc=1, device_id=(lax.rem(me + off, TA), g), device_id_type=MESH
        )
        return carry

    lax.fori_loop(1, TA, greet, 0)
    pl.semaphore_signal(gate, inc=1, device_id=(left_ta, left_gx), device_id_type=MESH)
    pl.semaphore_signal(gate, inc=1, device_id=(right_ta, right_gx), device_id_type=MESH)
    pl.semaphore_wait(gate, TA + 1)

    constants = [
        pltpu.make_async_copy(src, dst, const_sem.at[n])
        for n, (src, dst) in enumerate(
            [
                (coupling_in, coupling),
                (diffraction_in, diffraction),
                (dft_in, dft),
                (twist_in, twist),
                (within_in, within),
                (before_in, before),
            ]
        )
    ]
    for copy in constants:
        copy.start()

    place = pl.ds(pl.multiple_of(me * 32, 32), 32)
    for step in range(ROWS):

        def send(off, carry, step=step):
            to = lax.rem(me + off, TA)
            row = row_at(step, lax.rem(to, 2))
            pltpu.make_async_remote_copy(
                src_ref=field.at[:, 4 * to + row],
                dst_ref=rx.at[row, :, place],
                send_sem=send_sem.at[step],
                recv_sem=recv_sem.at[step],
                device_id=(to, g),
                device_id_type=MESH,
            ).start()
            return carry

        lax.fori_loop(1, TA, send, 0)
        own = row_at(step, odd)
        pltpu.make_async_copy(
            field.at[:, 4 * me + own], rx.at[own, :, place], recv_sem.at[step]
        ).start()

    @pl.when(jnp.logical_not(has_left))
    def _():
        fe[0:2] = jnp.zeros((2, 2, Y * R, R), F32)

    @pl.when(jnp.logical_not(has_right))
    def _():
        fe[6:8] = jnp.zeros((2, 2, Y * R, R), F32)

    for copy in constants:
        copy.wait()

    def halo_copy(row, to_left):
        return pltpu.make_async_remote_copy(
            src_ref=fe.at[row + 2],
            dst_ref=fe.at[lax.rem(row + 6, 8)],
            send_sem=halo_send.at[row],
            recv_sem=halo_recv.at[row],
            device_id=(left_ta, left_gx) if to_left else (right_ta, right_gx),
            device_id_type=MESH,
        )

    def transform(groups):
        real = jnp.concatenate([re for re, _ in groups], axis=1)
        imag = jnp.concatenate([im for _, im in groups], axis=1)
        high, low = halves(jnp.concatenate([real, imag], axis=0))
        table = dft[...]
        section = dot(table, jnp.concatenate([high, high, low], axis=0))
        cos, sin = twist[0], twist[1]
        turned = []
        for n in range(len(groups)):
            re = section[:R, n * R : (n + 1) * R]
            im = section[R:, n * R : (n + 1) * R]
            turned.append(
                jnp.concatenate([re * cos - im * sin, re * sin + im * cos], axis=1)
            )
        high, low = halves(jnp.concatenate(turned, axis=0))
        final = dot_nt(table, jnp.concatenate([high, high, low], axis=1))
        return [
            (final[:R, n * R : (n + 1) * R], final[R:, n * R : (n + 1) * R])
            for n in range(len(groups))
        ]

    def pair(row, p):
        groups_e, groups_n = [], []
        for side in range(2):
            y = 2 * p + side
            re = rx[row, 0, pl.ds(y, R, stride=Y), :]
            im = rx[row, 1, pl.ds(y, R, stride=Y), :]
            intensity = re * re + im * im
            rate = ion_ref[4 * me + row, y] * jnp.exp(-BARRIER * lax.rsqrt(intensity + 1.0))
            sums = dot(jnp.concatenate(halves(rate), axis=1), within[...])
            earlier = dot(before[...], jnp.concatenate(halves(sums[:, R:]), axis=0))
            plasma = 1.0 - jnp.exp(-(sums[:, :R] + earlier))
            groups_e.append((re, im))
            kerr = KERR * intensity
            groups_n.append((-kerr * im - plasma * re, kerr * re - plasma * im))
        spectra = transform(groups_e + groups_n)
        c = coupling[...]
        for side in range(2):
            at = pl.ds(pl.multiple_of((2 * p + side) * R, R), R)
            e_re, e_im = spectra[side]
            n_re, n_im = spectra[2 + side]
            fe[row + 2, 0, at, :] = e_re
            fe[row + 2, 1, at, :] = e_im
            part[row, 0, at, :] = e_re - c * n_im
            part[row, 1, at, :] = e_im + c * n_re

    for step in range(ROWS):
        row = row_at(step, odd)
        pltpu.make_async_copy(rx.at[row], rx.at[row], recv_sem.at[step]).wait()

        def body(p, carry, row=row):
            pair(row, p)
            return carry

        lax.fori_loop(0, Y // 2, body, 0)

        @pl.when(jnp.logical_and(row < 2, has_left))
        def _(row=row):
            halo_copy(row, True).start()

        @pl.when(jnp.logical_and(row >= 2, has_right))
        def _(row=row):
            halo_copy(row, False).start()

    def arrived(row):
        pltpu.make_async_copy(
            fe.at[lax.rem(row + 6, 8)], fe.at[lax.rem(row + 6, 8)], halo_recv.at[row]
        ).wait()

    def left_arrived():
        @pl.when(has_left)
        def _():
            arrived(2)
            arrived(3)

    def right_arrived():
        @pl.when(has_right)
        def _():
            arrived(0)
            arrived(1)

    def finish(row):
        def block(n, carry):
            k = pl.multiple_of(n * 8, 8)
            d = diffraction[pl.ds(k, 8), :] * (1.0 / 12.0)
            lap = []
            for c in range(2):
                mid = [fe[row + 2, c, pl.ds(y * R + k, 8), :] for y in range(Y)]
                planes = []
                for y in range(Y):
                    at = pl.ds(y * R + k, 8)
                    near = fe[row + 1, c, at, :] + fe[row + 3, c, at, :]
                    far = fe[row, c, at, :] + fe[row + 4, c, at, :]
                    for o in (-1, 1):
                        if 0 <= y + o < Y:
                            near = near + mid[y + o]
                    for o in (-2, 2):
                        if 0 <= y + o < Y:
                            far = far + mid[y + o]
                    planes.append(16.0 * near - far - 60.0 * mid[y])
                lap.append(planes)
            for y in range(Y):
                at = pl.ds(y * R + k, 8)
                to = pl.ds(k * Y + y, 8, stride=Y)
                result[row, 0, to, :] = part[row, 0, at, :] - d * lap[1][y]
                result[row, 1, to, :] = part[row, 1, at, :] + d * lap[0][y]
            return carry

        lax.fori_loop(0, R // 8, block, 0)
        copy = pltpu.make_async_copy(result.at[row], out.at[:, row], out_sem.at[row])
        copy.start()

    @pl.when(odd == 0)
    def _():
        left_arrived()

    @pl.when(odd == 1)
    def _():
        right_arrived()

    for step in range(2):
        finish(row_at(step, odd))

    @pl.when(odd == 0)
    def _():
        right_arrived()

    @pl.when(odd == 1)
    def _():
        left_arrived()

    for step in range(2, ROWS):
        finish(row_at(step, odd))

    for row in range(ROWS):
        pltpu.make_async_copy(result.at[row], out.at[:, row], out_sem.at[row]).wait()
    for step in range(ROWS):
        sent = rx.at[0, :, pl.ds(0, (TA - 1) * 32)]
        pltpu.make_async_copy(sent, sent, send_sem.at[step]).wait()
    for row in range(ROWS):

        @pl.when(has_left if row < 2 else has_right)
        def _(row=row):
            halo_copy(row, row < 2).wait_send()


def on_device(field, ion_rate, diffraction, coupling):
    x_rows = field.shape[1]
    tiles = field.reshape(2, x_rows, Y, 4, R).transpose(0, 1, 3, 2, 4).reshape(2, x_rows, 32, R)
    dft, twist, within, before = tables()
    hbm = pl.BlockSpec(memory_space=pl.ANY)
    spectrum = pl.pallas_call(
        kernel,
        out_shape=jax.ShapeDtypeStruct((2, ROWS, R * Y, R), F32),
        in_specs=[pl.BlockSpec(memory_space=pltpu.SMEM)] + [hbm] * 7,
        out_specs=hbm,
        scratch_shapes=[
            pltpu.VMEM((ROWS, 2, R * Y, R), F32),
            pltpu.VMEM((ROWS + 4, 2, Y * R, R), F32),
            pltpu.VMEM((ROWS, 2, Y * R, R), F32),
            pltpu.VMEM((ROWS, 2, R * Y, R), F32),
            pltpu.VMEM((R, R), F32),
            pltpu.VMEM((R, R), F32),
            pltpu.VMEM(dft.shape, BF16),
            pltpu.VMEM(twist.shape, F32),
            pltpu.VMEM(within.shape, BF16),
            pltpu.VMEM(before.shape, BF16),
            pltpu.SemaphoreType.DMA((6,)),
            pltpu.SemaphoreType.DMA((ROWS,)),
            pltpu.SemaphoreType.DMA((ROWS,)),
            pltpu.SemaphoreType.DMA((ROWS,)),
            pltpu.SemaphoreType.DMA((ROWS,)),
            pltpu.SemaphoreType.DMA((ROWS,)),
        ],
        compiler_params=pltpu.CompilerParams(
            collective_id=0, has_side_effects=True, vmem_limit_bytes=48 * 1024 * 1024
        ),
    )(
        ion_rate,
        tiles,
        coupling.reshape(R, R),
        diffraction.reshape(R, R),
        jnp.asarray(dft),
        jnp.asarray(twist),
        jnp.asarray(within),
        jnp.asarray(before),
    )
    spectrum = spectrum.reshape(2, ROWS, R, Y, R).transpose(0, 1, 3, 2, 4)
    return spectrum.reshape(2, ROWS, Y, R * R)


def solution(mesh):
    in_specs = (P(None, "gx", None, "ta"), P("gx", None), P(), P())
    out_specs = P(None, ("gx", "ta"), None, None)
    return jax.shard_map(
        on_device, mesh=mesh, in_specs=in_specs, out_specs=out_specs, check_vma=False
    )
```

```python
import math

import jax
import jax.numpy as jnp
import ml_dtypes
import numpy as np
from jax import lax
from jax.experimental import pallas as pl
from jax.experimental.pallas import tpu as pltpu
from jax.sharding import PartitionSpec as P

BARRIER = 2.0
KERR = 0.5
MESH = pl.DeviceIdType.MESH
R = 128
TA = 32
GX = 4
LINES = 4
COLS = 4
ROWS = 4
Y = 8
F32 = jnp.float32
BF16 = jnp.bfloat16
INNER, OWN, NEAR, FAR, AHEAD, FORWARD = 0, 2, 4, 5, 6, 7


def tables():
    index = np.arange(R)
    angle = 2.0 * np.pi / R * (np.outer(index, index) % R)
    cos, sin = np.cos(angle), np.sin(angle)
    full = np.block([[cos, sin], [-sin, cos]]).astype(np.float32)
    high = full.astype(ml_dtypes.bfloat16)
    low = (full - high.astype(np.float32)).astype(ml_dtypes.bfloat16)
    dft = np.concatenate([high, low, high], axis=1)
    turn = 2.0 * np.pi / (R * R) * np.outer(index, index)
    twist = np.stack([np.cos(turn), -np.sin(turn)]) / R
    upper = (index[:, None] <= index[None, :]).astype(np.float32)
    within = np.concatenate([upper, np.ones((R, R), np.float32)], axis=1)
    within = np.concatenate([within, within], axis=0)
    lower = (index[:, None] > index[None, :]).astype(np.float32)
    before = np.concatenate([lower, lower], axis=1)
    return (
        dft,
        twist.astype(np.float32),
        within.astype(ml_dtypes.bfloat16),
        before.astype(ml_dtypes.bfloat16),
    )


def halves(v):
    high = v.astype(BF16)
    return high, (v - high.astype(F32)).astype(BF16)


def dot(a, b):
    return jnp.dot(a, b, preferred_element_type=F32)


def dot_nt(a, b):
    return lax.dot_general(a, b, (((1,), (1,)), ((), ())), preferred_element_type=F32)


def kernel(
    ion_in, field, coupling_in, diffraction_in, dft_in, twist_in, within_in, before_in,
    out,
    rx, fe, part, result, ion_ref, coupling, diffraction, dft, twist, within, before,
    const_sem, send_sem, recv_sem, cross_sem, swap_send, swap_recv, out_sem,
):
    me = lax.axis_index("ta")
    g = lax.axis_index("gx")
    odd = lax.rem(me, 2)
    chip = me // 2
    col = lax.rem(chip, COLS)
    line = chip // COLS
    first = me == 0
    last = me == TA - 1
    paired = jnp.logical_not(
        jnp.logical_or(jnp.logical_and(first, g == 0), jnp.logical_and(last, g == GX - 1))
    )
    partner = lax.rem(jnp.where(odd == 0, me + TA - 1, me + 1), TA)
    partner_gx = lax.rem(jnp.where(first, g + GX - 1, jnp.where(last, g + 1, g)), GX)

    gate = pltpu.get_barrier_semaphore()

    def greet(device):
        pl.semaphore_signal(gate, inc=1, device_id=device, device_id_type=MESH)

    def greet_plane(off, carry):
        greet((lax.rem(me + off, TA), g))
        return carry

    lax.fori_loop(1, TA, greet_plane, 0)

    def greet_next(at, carry):
        greet((at, lax.rem(g + 1, GX)))
        return carry

    def greet_previous(at, carry):
        greet((at, lax.rem(g + GX - 1, GX)))
        return carry

    @pl.when(jnp.logical_and(last, g < GX - 1))
    def _():
        lax.fori_loop(0, TA, greet_next, 0)

    @pl.when(jnp.logical_and(first, g > 0))
    def _():
        lax.fori_loop(0, TA, greet_previous, 0)

    pl.semaphore_wait(gate, TA - 1 + jnp.where(g > 0, 1, 0) + jnp.where(g < GX - 1, 1, 0))

    constants = [
        pltpu.make_async_copy(src, dst, const_sem.at[n])
        for n, (src, dst) in enumerate(
            [
                (ion_in, ion_ref),
                (coupling_in, coupling),
                (diffraction_in, diffraction),
                (dft_in, dft),
                (twist_in, twist),
                (within_in, within),
                (before_in, before),
            ]
        )
    ]
    for copy in constants:
        copy.start()

    place = pl.ds(pl.multiple_of(me * 32, 32), 32)

    def send(to, plane, row, slot, count, kind, arrival=None, sem=None):
        pltpu.make_async_remote_copy(
            src_ref=field.at[:, pl.ds(row, count)],
            dst_ref=rx.at[:, pl.ds(slot, count), place],
            send_sem=send_sem.at[kind] if sem is None else sem,
            recv_sem=recv_sem.at[kind if arrival is None else arrival],
            device_id=(to, plane),
            device_id_type=MESH,
        ).start()

    def keep(row, slot, kind):
        pltpu.make_async_copy(
            field.at[:, pl.ds(row, 1)], rx.at[:, pl.ds(slot, 1), place], recv_sem.at[kind]
        ).start()

    def device_at(j, shift, core):
        y = lax.rem(line + j, LINES)
        return 8 * y + 2 * lax.rem(col + shift, COLS) + core

    def send_ahead(j, carry):
        for shift, core in ((3, 0), (1, 1)):
            to = device_at(j, shift, core)

            @pl.when(jnp.logical_and(to > 0, to < TA - 1))
            def _(to=to, core=core):
                send(to, g, 4 * to - 2 + 4 * core, 0, 4, AHEAD)

        return carry

    lax.fori_loop(0, LINES, send_ahead, 0)
    end = 4 * TA - 2
    above, below = lax.rem(g + 1, GX), lax.rem(g + GX - 1, GX)

    @pl.when(col == 1)
    def _():
        send(0, g, 0, 2, 2, AHEAD)

        @pl.when(g < GX - 1)
        def _():
            send(0, above, end, 0, 2, AHEAD)

        @pl.when(g == GX - 1)
        def _():
            send(TA - 1, g, end, 0, 2, AHEAD, FORWARD)

    @pl.when(col == 2)
    def _():
        send(TA - 1, g, end, 0, 2, AHEAD)

        @pl.when(g > 0)
        def _():
            send(TA - 1, below, 0, 2, 2, AHEAD)

        @pl.when(g == 0)
        def _():
            send(0, g, 0, 2, 2, AHEAD, FORWARD)

    for i in range(2):

        def send_inner(off, carry, i=i):
            to = lax.rem(me + off, TA)
            send(to, g, 4 * to + 2 * (1 - lax.rem(to, 2)) + i, 4 + i, 1, INNER + i)
            return carry

        lax.fori_loop(1, TA, send_inner, 0)
        keep(4 * me + 2 * (1 - odd) + i, 4 + i, INNER + i)

    @pl.when(jnp.logical_not(paired))
    def _():
        fe[pl.ds(6 * odd, 2)] = jnp.zeros((2, 2, Y * R, R), F32)

    def arrived(kind, slots, rows):
        ref = rx.at[:, pl.ds(0, slots), pl.ds(0, rows)]
        pltpu.make_async_copy(ref, ref, recv_sem.at[kind]).wait()

    @pl.when(paired)
    def _():
        arrived(AHEAD, 4, 256)

    @pl.when(jnp.logical_not(paired))
    def _():
        arrived(AHEAD, 2, 256)

    def forward(y, slots, rows):
        from_col = lax.rem(col + jnp.where(odd == 0, 1, 3), COLS)
        at = pl.ds(pl.multiple_of(256 * y + 64 * from_col, 64), 64)
        return pltpu.make_async_remote_copy(
            src_ref=rx.at[:, pl.ds(0, 4), at],
            dst_ref=rx.at[:, pl.ds(0, 4), at],
            send_sem=send_sem.at[FORWARD],
            recv_sem=recv_sem.at[FORWARD],
            device_id=(partner, partner_gx),
            device_id_type=MESH,
        )

    @pl.when(paired)
    def _():
        for y in range(LINES):
            forward(y, 4, 256).start()

    direct = ((0, 0), (0, 1), (1, 0), (3, 1))

    def row_of(to, core, kind):
        if kind < NEAR:
            i = kind - OWN
            return (4 * to + i, 2 + i) if core == 0 else (4 * to + 2 + i, i)
        if kind == NEAR:
            return (4 * to - 1, 1) if core == 0 else (4 * to + 4, 2)
        return (4 * to - 2, 0) if core == 0 else (4 * to + 5, 3)

    for kind in (OWN, OWN + 1, NEAR, FAR):

        def send_direct(j, carry, kind=kind):
            for shift, core in direct:
                to = device_at(j, shift, core)
                row, slot = row_of(to, core, kind)
                allowed = to != me
                if kind >= NEAR:
                    allowed = jnp.logical_and(allowed, to != (0 if core == 0 else TA - 1))

                @pl.when(allowed)
                def _(to=to, row=row, slot=slot):
                    send(to, g, row, slot, 1, kind)

            return carry

        lax.fori_loop(0, LINES, send_direct, 0)
        if kind >= NEAR:
            at_end = jnp.logical_or(col == 0, col == 3)
            i = kind - NEAR

            @pl.when(jnp.logical_and(at_end, g < GX - 1))
            def _(kind=kind, i=i):
                send(0, above, end + 1 - i, 1 - i, 1, kind, sem=cross_sem.at[i])

            @pl.when(jnp.logical_and(at_end, g > 0))
            def _(kind=kind, i=i):
                send(TA - 1, below, i, 2 + i, 1, kind, sem=cross_sem.at[2 + i])

        for core in range(2):
            mine = odd == core
            if kind >= NEAR:
                mine = jnp.logical_and(mine, me != (0 if core == 0 else TA - 1))

            @pl.when(mine)
            def _(core=core, kind=kind):
                keep(*row_of(me, core, kind), kind)

    for copy in constants:
        copy.wait()

    def transform(groups):
        real = jnp.concatenate([re for re, _ in groups], axis=1)
        imag = jnp.concatenate([im for _, im in groups], axis=1)
        high, low = halves(jnp.concatenate([real, imag], axis=0))
        table = dft[...]
        section = dot(table, jnp.concatenate([high, high, low], axis=0))
        cos, sin = twist[0], twist[1]
        turned = []
        for n in range(len(groups)):
            re = section[:R, n * R : (n + 1) * R]
            im = section[R:, n * R : (n + 1) * R]
            turned.append(
                jnp.concatenate([re * cos - im * sin, re * sin + im * cos], axis=1)
            )
        high, low = halves(jnp.concatenate(turned, axis=0))
        final = dot_nt(table, jnp.concatenate([high, high, low], axis=1))
        return [
            (final[:R, n * R : (n + 1) * R], final[R:, n * R : (n + 1) * R])
            for n in range(len(groups))
        ]

    def series(slot, y):
        return tuple(rx[c, slot, pl.ds(y, R, stride=Y), :] for c in range(2))

    def plane_of(y):
        return pl.ds(pl.multiple_of(y * R, R), R)

    def own_pair(slot, where, p):
        groups_e, groups_n = [], []
        for side in range(2):
            y = 2 * p + side
            re, im = series(slot, y)
            intensity = re * re + im * im
            rate = ion_ref[y, 4 * me + where - 2] * jnp.exp(
                -BARRIER * lax.rsqrt(intensity + 1.0)
            )
            sums = dot(jnp.concatenate(halves(rate), axis=1), within[...])
            earlier = dot(before[...], jnp.concatenate(halves(sums[:, R:]), axis=0))
            plasma = 1.0 - jnp.exp(-(sums[:, :R] + earlier))
            groups_e.append((re, im))
            kerr = KERR * intensity
            groups_n.append((-kerr * im - plasma * re, kerr * re - plasma * im))
        spectra = transform(groups_e + groups_n)
        c = coupling[...]
        for side in range(2):
            at = plane_of(2 * p + side)
            e_re, e_im = spectra[side]
            n_re, n_im = spectra[2 + side]
            fe[where, 0, at, :] = e_re
            fe[where, 1, at, :] = e_im
            part[where - 2, 0, at, :] = e_re - c * n_im
            part[where - 2, 1, at, :] = e_im + c * n_re

    def halo_four(slot, where, p):
        spectra = transform([series(slot, 4 * p + side) for side in range(4)])
        for side in range(4):
            at = plane_of(4 * p + side)
            fe[where, 0, at, :], fe[where, 1, at, :] = spectra[side]

    def swap(i):
        where = 4 + i - 2 * odd
        return pltpu.make_async_remote_copy(
            src_ref=fe.at[where],
            dst_ref=fe.at[jnp.where(odd == 0, i, 6 + i)],
            send_sem=swap_send.at[i],
            recv_sem=swap_recv.at[i],
            device_id=(me + 1 - 2 * odd, g),
            device_id_type=MESH,
        )

    def own_row(step, carry):
        for i in range(2):

            @pl.when(step == i)
            def _(i=i):
                arrived(INNER + i, 1, 1024)

            @pl.when(step == 2 + i)
            def _(i=i):
                arrived(OWN + i, 1, 512)

        @pl.when(jnp.logical_and(step == 2, paired))
        def _():
            arrived(FORWARD, 4, 256)

        @pl.when(jnp.logical_and(step == 2, jnp.logical_not(paired)))
        def _():
            arrived(FORWARD, 2, 256)

        slot = jnp.where(step < 2, 4 + step, step - 2 * odd)
        where = jnp.where(step < 2, 4 + step - 2 * odd, step + 2 * odd)

        def body(p, carry):
            own_pair(slot, where, p)
            return carry

        lax.fori_loop(0, Y // 2, body, 0)
        for i in range(2):

            @pl.when(step == i)
            def _(i=i):
                swap(i).start()

        return carry

    lax.fori_loop(0, ROWS, own_row, 0)

    def finish(row):
        def block(n, carry):
            k = pl.multiple_of(n * 8, 8)
            d = diffraction[pl.ds(k, 8), :] * (1.0 / 12.0)
            lap = []
            for c in range(2):
                mid = [fe[row + 2, c, pl.ds(y * R + k, 8), :] for y in range(Y)]
                planes = []
                for y in range(Y):
                    at = pl.ds(y * R + k, 8)
                    near = fe[row + 1, c, at, :] + fe[row + 3, c, at, :]
                    far = fe[row, c, at, :] + fe[row + 4, c, at, :]
                    for o in (-1, 1):
                        if 0 <= y + o < Y:
                            near = near + mid[y + o]
                    for o in (-2, 2):
                        if 0 <= y + o < Y:
                            far = far + mid[y + o]
                    planes.append(16.0 * near - far - 60.0 * mid[y])
                lap.append(planes)
            for y in range(Y):
                at = pl.ds(y * R + k, 8)
                to = pl.ds(k * Y + y, 8, stride=Y)
                result[row, 0, to, :] = part[row, 0, at, :] - d * lap[1][y]
                result[row, 1, to, :] = part[row, 1, at, :] + d * lap[0][y]
            return carry

        lax.fori_loop(0, R // 8, block, 0)
        pltpu.make_async_copy(result.at[row], out.at[:, row], out_sem.at[row]).start()

    for i in range(2):
        swap(i).wait()

    def finish_inner(n, carry):
        finish(jnp.where(odd == 0, 3 - n, n))
        return carry

    lax.fori_loop(0, 2, finish_inner, 0)

    def finish_outer(n, carry):
        @pl.when(paired)
        def _():
            for i in range(2):

                @pl.when(n == i)
                def _(i=i):
                    arrived(NEAR + i, 1, 512)

            slot = jnp.where(odd == 0, 1 - n, 2 + n)

            def body(p, carry):
                halo_four(slot, slot + 4 * odd, p)
                return carry

            lax.fori_loop(0, Y // 4, body, 0)

        finish(jnp.where(odd == 0, 1 - n, 2 + n))
        return carry

    lax.fori_loop(0, 2, finish_outer, 0)

    def sent(kind, slots, rows):
        ref = rx.at[:, pl.ds(0, slots), pl.ds(0, rows)]
        pltpu.make_async_copy(ref, ref, send_sem.at[kind]).wait()

    sent(AHEAD, 4, 256)

    @pl.when(paired)
    def _():
        sent(FORWARD, 4, 256)

    for i in range(2):
        sent(INNER + i, 1, 31 * 32)
        sent(OWN + i, 1, 15 * 32)
        at_end = jnp.logical_or(col == 0, col == 3)
        tip = jnp.logical_or(first, last)

        @pl.when(jnp.logical_not(at_end))
        def _(i=i):
            sent(NEAR + i, 1, 15 * 32)

        @pl.when(tip)
        def _(i=i):
            sent(NEAR + i, 1, 14 * 32)

        @pl.when(jnp.logical_and(at_end, jnp.logical_not(tip)))
        def _(i=i):
            sent(NEAR + i, 1, 13 * 32)

        for n, there in enumerate((g < GX - 1, g > 0)):

            @pl.when(jnp.logical_and(at_end, there))
            def _(i=i, n=n):
                ref = rx.at[:, pl.ds(0, 1), pl.ds(0, 32)]
                pltpu.make_async_copy(ref, ref, cross_sem.at[2 * n + i]).wait()

    for row in range(ROWS):
        pltpu.make_async_copy(result.at[row], out.at[:, row], out_sem.at[row]).wait()


def on_device(field, ion_rate, diffraction, coupling):
    x_rows = field.shape[1]
    tiles = field.reshape(2, x_rows, Y, 4, R).transpose(0, 1, 3, 2, 4).reshape(2, x_rows, 32, R)
    dft, twist, within, before = tables()
    hbm = pl.BlockSpec(memory_space=pl.ANY)
    spectrum = pl.pallas_call(
        kernel,
        out_shape=jax.ShapeDtypeStruct((2, ROWS, R * Y, R), F32),
        in_specs=[hbm] * 8,
        out_specs=hbm,
        scratch_shapes=[
            pltpu.VMEM((2, ROWS + 2, R * Y, R), F32),
            pltpu.VMEM((ROWS + 4, 2, Y * R, R), F32),
            pltpu.VMEM((ROWS, 2, Y * R, R), F32),
            pltpu.VMEM((ROWS, 2, R * Y, R), F32),
            pltpu.SMEM((Y, x_rows), F32),
            pltpu.VMEM((R, R), F32),
            pltpu.VMEM((R, R), F32),
            pltpu.VMEM(dft.shape, BF16),
            pltpu.VMEM(twist.shape, F32),
            pltpu.VMEM(within.shape, BF16),
            pltpu.VMEM(before.shape, BF16),
            pltpu.SemaphoreType.DMA((7,)),
            pltpu.SemaphoreType.DMA((8,)),
            pltpu.SemaphoreType.DMA((8,)),
            pltpu.SemaphoreType.DMA((4,)),
            pltpu.SemaphoreType.DMA((2,)),
            pltpu.SemaphoreType.DMA((2,)),
            pltpu.SemaphoreType.DMA((ROWS,)),
        ],
        compiler_params=pltpu.CompilerParams(
            collective_id=0, has_side_effects=True, vmem_limit_bytes=60 * 1024 * 1024
        ),
    )(
        ion_rate.T,
        tiles,
        coupling.reshape(R, R),
        diffraction.reshape(R, R),
        jnp.asarray(dft),
        jnp.asarray(twist),
        jnp.asarray(within),
        jnp.asarray(before),
    )
    spectrum = spectrum.reshape(2, ROWS, R, Y, R).transpose(0, 1, 3, 2, 4)
    return spectrum.reshape(2, ROWS, Y, R * R)


def solution(mesh):
    in_specs = (P(None, "gx", None, "ta"), P("gx", None), P(), P())
    out_specs = P(None, ("gx", "ta"), None, None)
    return jax.shard_map(
        on_device, mesh=mesh, in_specs=in_specs, out_specs=out_specs, check_vma=False
    )
```

```python
import math

import jax
import jax.numpy as jnp
import ml_dtypes
import numpy as np
from jax import lax
from jax.experimental import pallas as pl
from jax.experimental.pallas import tpu as pltpu
from jax.sharding import PartitionSpec as P

BARRIER = 2.0
KERR = 0.5
MESH = pl.DeviceIdType.MESH
R = 128
TA = 32
GX = 4
ROWS = 4
Y = 8
PIECES = 4
F32 = jnp.float32
BF16 = jnp.bfloat16


def tables():
    index = np.arange(R)
    angle = 2.0 * np.pi / R * (np.outer(index, index) % R)
    cos, sin = np.cos(angle), np.sin(angle)
    full = np.block([[cos, sin], [-sin, cos]]).astype(np.float32)
    high = full.astype(ml_dtypes.bfloat16)
    low = (full - high.astype(np.float32)).astype(ml_dtypes.bfloat16)
    dft = np.concatenate([high, low, high], axis=1)
    turn = 2.0 * np.pi / (R * R) * np.outer(index, index)
    twist = np.stack([np.cos(turn), -np.sin(turn)]) / R
    upper = (index[:, None] <= index[None, :]).astype(np.float32)
    within = np.concatenate([upper, np.ones((R, R), np.float32)], axis=1)
    within = np.concatenate([within, within], axis=0)
    lower = (index[:, None] > index[None, :]).astype(np.float32)
    before = np.concatenate([lower, lower], axis=1)
    return (
        dft,
        twist.astype(np.float32),
        within.astype(ml_dtypes.bfloat16),
        before.astype(ml_dtypes.bfloat16),
    )


def halves(v):
    high = v.astype(BF16)
    return high, (v - high.astype(F32)).astype(BF16)


def dot(a, b):
    return jnp.dot(a, b, preferred_element_type=F32)


def dot_nt(a, b):
    return lax.dot_general(a, b, (((1,), (1,)), ((), ())), preferred_element_type=F32)


def kernel(
    ion_in, field, coupling_in, diffraction_in, dft_in, twist_in, within_in, before_in,
    q_out, halo_out,
    rx, fe, part, result, blank, ion_ref, coupling, diffraction, dft, twist, within, before,
    const_sem, send_sem, recv_sem, halo_send, halo_recv, blank_sem, out_sem,
):
    me = lax.axis_index("ta")
    g = lax.axis_index("gx")
    odd = lax.rem(me, 2)
    has_left = jnp.logical_or(me > 0, g > 0)
    has_right = jnp.logical_or(me < TA - 1, g < GX - 1)
    left_ta = lax.rem(me + TA - 1, TA)
    left_gx = lax.rem(jnp.where(me == 0, g + GX - 1, g), GX)
    right_ta = lax.rem(me + 1, TA)
    right_gx = lax.rem(jnp.where(me == TA - 1, g + 1, g), GX)

    def row_at(step, parity):
        return jnp.where(parity == 0, step, ROWS - 1 - step)

    gate = pltpu.get_barrier_semaphore()

    def greet(off, carry):
        pl.semaphore_signal(
            gate, inc=1, device_id=(lax.rem(me + off, TA), g), device_id_type=MESH
        )
        return carry

    lax.fori_loop(1, TA, greet, 0)
    pl.semaphore_signal(gate, inc=1, device_id=(left_ta, left_gx), device_id_type=MESH)
    pl.semaphore_signal(gate, inc=1, device_id=(right_ta, right_gx), device_id_type=MESH)
    pl.semaphore_wait(gate, TA + 1)

    constants = [
        pltpu.make_async_copy(src, dst, const_sem.at[n])
        for n, (src, dst) in enumerate(
            [
                (ion_in, ion_ref),
                (coupling_in, coupling),
                (diffraction_in, diffraction),
                (dft_in, dft),
                (twist_in, twist),
                (within_in, within),
                (before_in, before),
            ]
        )
    ]
    for copy in constants:
        copy.start()

    place = pl.ds(pl.multiple_of(me * 32, 32), 32)
    def send(to, step):
        row = row_at(step, lax.rem(to, 2))
        pltpu.make_async_remote_copy(
            src_ref=field.at[:, 4 * to + row],
            dst_ref=rx.at[row, :, place],
            send_sem=send_sem.at[step],
            recv_sem=recv_sem.at[step],
            device_id=(to, g),
            device_id_type=MESH,
        ).start()

    def send_ends(j, carry):
        for at in (0, 7):
            to = 8 * lax.rem(me // 8 + j, 4) + at

            @pl.when(to != me)
            def _(to=to):
                send(to, 0)
                send(to, 1)

        return carry

    lax.fori_loop(0, 4, send_ends, 0)

    for step in range(ROWS):

        def send_row(off, carry, step=step):
            to = lax.rem(me + off, TA)
            if step < 2:
                at = lax.rem(to, 8)

                @pl.when(jnp.logical_and(at > 0, at < 7))
                def _():
                    send(to, step)

            else:
                send(to, step)
            return carry

        lax.fori_loop(1, TA, send_row, 0)
        own = row_at(step, odd)
        pltpu.make_async_copy(
            field.at[:, 4 * me + own], rx.at[own, :, place], recv_sem.at[step]
        ).start()

    def blank_copy(slot):
        return pltpu.make_async_copy(blank, halo_out.at[slot], blank_sem.at[slot])

    @pl.when(jnp.logical_not(has_left))
    def _():
        blank[...] = jnp.zeros_like(blank)
        blank_copy(0).start()
        blank_copy(1).start()

    @pl.when(jnp.logical_not(has_right))
    def _():
        blank[...] = jnp.zeros_like(blank)
        blank_copy(2).start()
        blank_copy(3).start()

    for copy in constants:
        copy.wait()

    def halo_copy(row, to_left):
        return pltpu.make_async_remote_copy(
            src_ref=fe.at[row],
            dst_ref=halo_out.at[lax.rem(row + 2, ROWS)],
            send_sem=halo_send.at[row],
            recv_sem=halo_recv.at[row],
            device_id=(left_ta, left_gx) if to_left else (right_ta, right_gx),
            device_id_type=MESH,
        )

    def transform(groups):
        real = jnp.concatenate([re for re, _ in groups], axis=1)
        imag = jnp.concatenate([im for _, im in groups], axis=1)
        high, low = halves(jnp.concatenate([real, imag], axis=0))
        table = dft[...]
        section = dot(table, jnp.concatenate([high, high, low], axis=0))
        cos, sin = twist[0], twist[1]
        turned = []
        for n in range(len(groups)):
            re = section[:R, n * R : (n + 1) * R]
            im = section[R:, n * R : (n + 1) * R]
            turned.append(
                jnp.concatenate([re * cos - im * sin, re * sin + im * cos], axis=1)
            )
        high, low = halves(jnp.concatenate(turned, axis=0))
        final = dot_nt(table, jnp.concatenate([high, high, low], axis=1))
        return [
            (final[:R, n * R : (n + 1) * R], final[R:, n * R : (n + 1) * R])
            for n in range(len(groups))
        ]

    def pair(row, p):
        groups_e, groups_n = [], []
        for side in range(2):
            y = 2 * p + side
            re = rx[row, 0, pl.ds(y, R, stride=Y), :]
            im = rx[row, 1, pl.ds(y, R, stride=Y), :]
            intensity = re * re + im * im
            rate = ion_ref[y, 4 * me + row] * jnp.exp(-BARRIER * lax.rsqrt(intensity + 1.0))
            sums = dot(jnp.concatenate(halves(rate), axis=1), within[...])
            earlier = dot(before[...], jnp.concatenate(halves(sums[:, R:]), axis=0))
            plasma = 1.0 - jnp.exp(-(sums[:, :R] + earlier))
            groups_e.append((re, im))
            kerr = KERR * intensity
            groups_n.append((-kerr * im - plasma * re, kerr * re - plasma * im))
        spectra = transform(groups_e + groups_n)
        c = coupling[...]
        for side in range(2):
            at = pl.ds(pl.multiple_of((2 * p + side) * R, R), R)
            e_re, e_im = spectra[side]
            n_re, n_im = spectra[2 + side]
            fe[row, 0, at, :] = e_re
            fe[row, 1, at, :] = e_im
            part[row, 0, at, :] = e_re - c * n_im
            part[row, 1, at, :] = e_im + c * n_re

    def own_row(step, carry):
        row = row_at(step, odd)
        pltpu.make_async_copy(rx.at[row], rx.at[row], recv_sem.at[step]).wait()

        def body(p, carry):
            pair(row, p)
            return carry

        lax.fori_loop(0, Y // 2, body, 0, unroll=4)

        @pl.when(jnp.logical_and(row < 2, has_left))
        def _():
            halo_copy(row, True).start()

        @pl.when(jnp.logical_and(row >= 2, has_right))
        def _():
            halo_copy(row, False).start()

        return carry

    lax.fori_loop(0, ROWS, own_row, 0)

    def inner_terms(row):
        def block(n, carry):
            k = pl.multiple_of(n * 8, 8)
            d = diffraction[pl.ds(k, 8), :] * (1.0 / 12.0)
            lap = []
            for c in range(2):
                mid = [fe[row, c, pl.ds(y * R + k, 8), :] for y in range(Y)]
                planes = []
                for y in range(Y):
                    at = pl.ds(y * R + k, 8)
                    near = [fe[row + o, c, at, :] for o in (-1, 1) if 0 <= row + o < ROWS]
                    near += [mid[y + o] for o in (-1, 1) if 0 <= y + o < Y]
                    far = [fe[row + o, c, at, :] for o in (-2, 2) if 0 <= row + o < ROWS]
                    far += [mid[y + o] for o in (-2, 2) if 0 <= y + o < Y]
                    planes.append(16.0 * sum(near[1:], near[0]) - sum(far[1:], far[0]) - 60.0 * mid[y])
                lap.append(planes)
            for y in range(Y):
                at = pl.ds(y * R + k, 8)
                to = pl.ds(k * Y + y, 8, stride=Y)
                result[row, 0, to, :] = part[row, 0, at, :] - d * lap[1][y]
                result[row, 1, to, :] = part[row, 1, at, :] + d * lap[0][y]
            return carry

        lax.fori_loop(0, R // 8, block, 0)
        pltpu.make_async_copy(result.at[row], q_out.at[:, row], out_sem.at[row]).start()

    for row in range(ROWS):
        inner_terms(row)

    for row in range(ROWS):
        pltpu.make_async_copy(result.at[row], q_out.at[:, row], out_sem.at[row]).wait()
    for step in range(ROWS):
        sent = rx.at[0, :, pl.ds(0, (TA - 1) * 32)]
        pltpu.make_async_copy(sent, sent, send_sem.at[step]).wait()
    for row in range(ROWS):

        @pl.when(has_left if row < 2 else has_right)
        def _(row=row):
            halo_copy(row, row < 2).wait_send()

    for row in range(ROWS):
        slot = (row + 2) % ROWS
        there = has_right if row < 2 else has_left

        @pl.when(there)
        def _(row=row, slot=slot):
            pltpu.make_async_copy(halo_out.at[slot], halo_out.at[slot], halo_recv.at[row]).wait()

        @pl.when(jnp.logical_not(there))
        def _(slot=slot):
            blank_copy(slot).wait()


def add_halo(
    q_in, halo_in, diffraction_in, out,
    q, halo, diffraction, result, q_sem, halo_sem, d_sem, out_sem,
):
    depth = R // PIECES

    def copies(n):
        wide = pl.ds(n * depth * Y, depth * Y)
        thin = pl.ds(n * depth, depth)
        return (
            pltpu.make_async_copy(q_in.at[:, :, wide], q.at[:, :, wide], q_sem.at[n]),
            pltpu.make_async_copy(
                halo_in.at[:, :, :, thin], halo.at[:, :, :, thin], halo_sem.at[n]
            ),
            pltpu.make_async_copy(result.at[:, :, wide], out.at[:, :, wide], out_sem.at[n]),
        )

    first = pltpu.make_async_copy(diffraction_in, diffraction, d_sem)
    first.start()
    for n in range(PIECES):
        for copy in copies(n)[:2]:
            copy.start()
    first.wait()
    for n in range(PIECES):
        for copy in copies(n)[:2]:
            copy.wait()

        def block(i, carry, n=n):
            k = pl.multiple_of(n * depth + 8 * i, 8)
            at_k = pl.ds(k, 8)
            d = diffraction[at_k, :] * (1.0 / 12.0)
            for y in range(Y):
                lap = []
                for c in range(2):
                    h = [halo[slot, c, y, at_k, :] for slot in range(4)]
                    lap.append((16.0 * h[1] - h[0], -h[1], -h[2], 16.0 * h[2] - h[3]))
                at = pl.ds(k * Y + y, 8, stride=Y)
                for row in range(ROWS):
                    result[0, row, at, :] = q[0, row, at, :] - d * lap[1][row]
                    result[1, row, at, :] = q[1, row, at, :] + d * lap[0][row]
            return carry

        lax.fori_loop(0, depth // 8, block, 0)
        copies(n)[2].start()
    for n in range(PIECES):
        copies(n)[2].wait()


def on_device(field, ion_rate, diffraction, coupling):
    x_rows = field.shape[1]
    tiles = field.reshape(2, x_rows, Y, 4, R).transpose(0, 1, 3, 2, 4).reshape(2, x_rows, 32, R)
    dft, twist, within, before = tables()
    hbm = pl.BlockSpec(memory_space=pl.ANY)
    q, halo = pl.pallas_call(
        kernel,
        out_shape=[
            jax.ShapeDtypeStruct((2, ROWS, R * Y, R), F32),
            jax.ShapeDtypeStruct((4, 2, Y * R, R), F32),
        ],
        in_specs=[hbm] * 8,
        out_specs=[hbm, hbm],
        scratch_shapes=[
            pltpu.VMEM((ROWS, 2, R * Y, R), F32),
            pltpu.VMEM((ROWS, 2, Y * R, R), F32),
            pltpu.VMEM((ROWS, 2, Y * R, R), F32),
            pltpu.VMEM((ROWS, 2, R * Y, R), F32),
            pltpu.VMEM((2, Y * R, R), F32),
            pltpu.SMEM((Y, x_rows), F32),
            pltpu.VMEM((R, R), F32),
            pltpu.VMEM((R, R), F32),
            pltpu.VMEM(dft.shape, BF16),
            pltpu.VMEM(twist.shape, F32),
            pltpu.VMEM(within.shape, BF16),
            pltpu.VMEM(before.shape, BF16),
            pltpu.SemaphoreType.DMA((7,)),
            pltpu.SemaphoreType.DMA((ROWS,)),
            pltpu.SemaphoreType.DMA((ROWS,)),
            pltpu.SemaphoreType.DMA((ROWS,)),
            pltpu.SemaphoreType.DMA((ROWS,)),
            pltpu.SemaphoreType.DMA((ROWS,)),
            pltpu.SemaphoreType.DMA((ROWS,)),
        ],
        compiler_params=pltpu.CompilerParams(
            collective_id=0, has_side_effects=True, vmem_limit_bytes=60 * 1024 * 1024
        ),
    )(
        ion_rate.T,
        tiles,
        coupling.reshape(R, R),
        diffraction.reshape(R, R),
        jnp.asarray(dft),
        jnp.asarray(twist),
        jnp.asarray(within),
        jnp.asarray(before),
    )
    spectrum = pl.pallas_call(
        add_halo,
        out_shape=jax.ShapeDtypeStruct((2, ROWS, R * Y, R), F32),
        in_specs=[hbm] * 3,
        out_specs=hbm,
        scratch_shapes=[
            pltpu.VMEM((2, ROWS, R * Y, R), F32),
            pltpu.VMEM((4, 2, Y, R, R), F32),
            pltpu.VMEM((R, R), F32),
            pltpu.VMEM((2, ROWS, R * Y, R), F32),
            pltpu.SemaphoreType.DMA((PIECES,)),
            pltpu.SemaphoreType.DMA((PIECES,)),
            pltpu.SemaphoreType.DMA,
            pltpu.SemaphoreType.DMA((PIECES,)),
        ],
        compiler_params=pltpu.CompilerParams(vmem_limit_bytes=60 * 1024 * 1024),
    )(q, halo.reshape(4, 2, Y, R, R), diffraction.reshape(R, R))
    spectrum = spectrum.reshape(2, ROWS, R, Y, R).transpose(0, 1, 3, 2, 4)
    return spectrum.reshape(2, ROWS, Y, R * R)


def solution(mesh):
    in_specs = (P(None, "gx", None, "ta"), P("gx", None), P(), P())
    out_specs = P(None, ("gx", "ta"), None, None)
    return jax.shard_map(
        on_device, mesh=mesh, in_specs=in_specs, out_specs=out_specs, check_vma=False
    )
```

```python
import functools
import math

import jax
import jax.numpy as jnp
import ml_dtypes
import numpy as np
from jax import lax
from jax.experimental import pallas as pl
from jax.experimental.pallas import tpu as pltpu
from jax.sharding import PartitionSpec as P

BARRIER = 2.0
KERR = 0.5
MESH = pl.DeviceIdType.MESH
R = 128
TA = 32
GX = 4
ROWS = 4
Y = 8
LINES = 4
COLS = 4
INNER, THEIRS, OWN, AHEAD, NEAR, FAR = 0, 2, 3, 4, 5, 6
BOUNDARY_STEP = 1
FORWARD_STEP = 2
DETOUR = (2,)
COPY_AFTER = 1
PIECES = 4
F32 = jnp.float32
BF16 = jnp.bfloat16


def tables():
    index = np.arange(R)
    angle = 2.0 * np.pi / R * (np.outer(index, index) % R)
    cos, sin = np.cos(angle), np.sin(angle)
    full = np.block([[cos, sin], [-sin, cos]]).astype(np.float32)
    high = full.astype(ml_dtypes.bfloat16)
    low = (full - high.astype(np.float32)).astype(ml_dtypes.bfloat16)
    dft = np.concatenate([high, low, high], axis=1)
    turn = 2.0 * np.pi / (R * R) * np.outer(index, index)
    twist = np.stack([np.cos(turn), -np.sin(turn)]) / R
    upper = (index[:, None] <= index[None, :]).astype(np.float32)
    within = np.concatenate([upper, np.ones((R, R), np.float32)], axis=1)
    within = np.concatenate([within, within], axis=0)
    lower = (index[:, None] > index[None, :]).astype(np.float32)
    before = np.concatenate([lower, lower], axis=1)
    return (
        dft,
        twist.astype(np.float32),
        within.astype(ml_dtypes.bfloat16),
        before.astype(ml_dtypes.bfloat16),
    )


def detours(lines):
    return functools.reduce(jnp.logical_or, [lines == n for n in DETOUR])


def halves(v):
    high = v.astype(BF16)
    return high, (v - high.astype(F32)).astype(BF16)


def dot(a, b):
    return jnp.dot(a, b, preferred_element_type=F32)


def dot_nt(a, b):
    return lax.dot_general(a, b, (((1,), (1,)), ((), ())), preferred_element_type=F32)


def kernel(
    ion_in, field, coupling_in, diffraction_in, dft_in, twist_in, within_in, before_in,
    q_out, halo_out,
    rx, fe, part, result, side, ion_ref, coupling, diffraction, dft, twist, within, before,
    const_sem, send_sem, recv_sem, swap_send, swap_recv, halo_send, halo_recv, side_sem, out_sem,
):
    me = lax.axis_index("ta")
    g = lax.axis_index("gx")
    odd = lax.rem(me, 2)
    away = 1 - 2 * odd
    chip = me // 2
    col = lax.rem(chip, COLS)
    line = chip // COLS
    first, last = me == 0, me == TA - 1
    at_end = jnp.logical_or(lax.rem(me, 8) == 0, lax.rem(me, 8) == 7)
    plain = jnp.logical_not(at_end)
    tip = jnp.logical_or(jnp.logical_and(first, g == 0), jnp.logical_and(last, g == GX - 1))
    paired = jnp.logical_not(tip)
    cross = jnp.logical_and(paired, jnp.logical_or(first, last))
    spectral = jnp.logical_and(paired, at_end)
    wide = jnp.logical_or(
        jnp.logical_and(odd == 0, col == 1), jnp.logical_and(odd == 1, col == COLS - 2)
    )
    thin = jnp.logical_or(
        jnp.logical_and(odd == 1, col == 0), jnp.logical_and(odd == 0, col == COLS - 1)
    )
    even_share = jnp.logical_and(plain, jnp.logical_not(jnp.logical_or(wide, thin)))
    partner = lax.rem(me + TA - away, TA)
    partner_gx = jnp.where(first, lax.rem(g + GX - 1, GX), jnp.where(last, lax.rem(g + 1, GX), g))

    gate = pltpu.get_barrier_semaphore()

    def greet(off, carry):
        pl.semaphore_signal(
            gate, inc=1, device_id=(lax.rem(me + off, TA), g), device_id_type=MESH
        )
        return carry

    lax.fori_loop(1, TA, greet, 0)

    @pl.when(cross)
    def _():
        pl.semaphore_signal(gate, inc=1, device_id=(partner, partner_gx), device_id_type=MESH)

    pl.semaphore_wait(gate, TA - 1 + jnp.where(cross, 1, 0))

    constants = [
        pltpu.make_async_copy(src, dst, const_sem.at[n])
        for n, (src, dst) in enumerate(
            [
                (ion_in, ion_ref),
                (coupling_in, coupling),
                (diffraction_in, diffraction),
                (dft_in, dft),
                (twist_in, twist),
                (within_in, within),
                (before_in, before),
            ]
        )
    ]
    for copy in constants:
        copy.start()

    place = pl.ds(pl.multiple_of(me * 32, 32), 32)

    def send(to, row, slot, count, kind):
        pltpu.make_async_remote_copy(
            src_ref=field.at[:, pl.ds(row, count)],
            dst_ref=rx.at[:, pl.ds(slot, count), place],
            send_sem=send_sem.at[kind],
            recv_sem=recv_sem.at[kind],
            device_id=(to, g),
            device_id_type=MESH,
        ).start()

    def keep(row, slot, count, kind):
        pltpu.make_async_copy(
            field.at[:, pl.ds(row, count)],
            rx.at[:, pl.ds(slot, count), place],
            recv_sem.at[kind],
        ).start()

    def deliver(act, core, kind, to):
        if kind == OWN:
            act(4 * to + 2 * core, 2 - 2 * core, 2, OWN)
        else:
            act(4 * to - 2 + 6 * core, 2 * core, 2, THEIRS)

    def boundary_sends(kind):
        def at_line(j, carry):
            y = lax.rem(line + j, LINES)
            detour = detours(lax.rem(LINES - j, LINES))
            for shift, core in ((2, 0), (2, 1), (3, 0), (1, 1), (0, 0), (0, 1)):
                column = lax.rem(col + shift, COLS)
                to = 8 * y + 2 * column + core
                fits = column != (0 if core == 0 else COLS - 1)
                if shift == 2:
                    fits = jnp.logical_and(col == (COLS - 1 if core == 0 else 0), detour)
                if shift in (1, 3):
                    far = column == (COLS - 1 if core == 0 else 0)
                    fits = jnp.logical_and(fits, jnp.logical_not(jnp.logical_and(far, detour)))
                if shift == 0:
                    fits = jnp.logical_and(fits, to != me)

                @pl.when(fits)
                def _(to=to, core=core):
                    deliver(functools.partial(send, to), core, kind, to)

            return carry

        lax.fori_loop(0, LINES, at_line, 0)
        for core in range(2):

            @pl.when(jnp.logical_and(plain, odd == core))
            def _(core=core):
                deliver(keep, core, kind, me)

    def end_sends():
        def at_line(j, carry):
            y = lax.rem(line + j, LINES)
            for to, core in ((8 * y, 0), (8 * y + 7, 1)):

                @pl.when(to != me)
                def _(to=to, core=core):
                    deliver(functools.partial(send, to), core, OWN, to)

            return carry

        lax.fori_loop(0, LINES, at_line, 0)
        for core in range(2):

            @pl.when(jnp.logical_and(at_end, odd == core))
            def _(core=core):
                deliver(keep, core, OWN, me)

    def inner_sends(i):
        def send_inner(off, carry):
            to = lax.rem(me + off, TA)
            send(to, 4 * to + 2 * (1 - lax.rem(to, 2)) + i, 4 + i, 1, INNER + i)
            return carry

        lax.fori_loop(1, TA, send_inner, 0)
        keep(4 * me + 2 * (1 - odd) + i, 4 + i, 1, INNER + i)

    def wait_for(sem, slots, rows):
        ref = rx.at[:, pl.ds(0, slots), pl.ds(0, rows)]
        pltpu.make_async_copy(ref, ref, sem).wait()

    def share(action, of_partner=False):
        more, less = 512 + 64 * len(DETOUR), 512 - 64 * len(DETOUR)
        for when, rows in (
            (even_share, 512),
            (thin if of_partner else wide, more),
            (wide if of_partner else thin, less),
        ):

            @pl.when(when)
            def _(rows=rows):
                action(rows)

    def forward(slot, count, kind):
        def one(column, y):
            at = pl.ds(pl.multiple_of(256 * y + 64 * column, 64), 64)
            pltpu.make_async_remote_copy(
                src_ref=rx.at[:, pl.ds(slot, count), at],
                dst_ref=rx.at[:, pl.ds(slot, count), at],
                send_sem=send_sem.at[kind],
                recv_sem=recv_sem.at[kind],
                device_id=(partner, partner_gx),
                device_id_type=MESH,
            ).start()

        def at_line(y, carry):
            detour = detours(lax.rem(y - line + LINES, LINES))
            one(col, y)

            @pl.when(jnp.logical_not(jnp.logical_and(thin, detour)))
            def _():
                one(lax.rem(col + jnp.where(odd == 0, 1, 3), COLS), y)

            @pl.when(jnp.logical_and(wide, detour))
            def _():
                one(lax.rem(col + 2, COLS), y)

            return carry

        lax.fori_loop(0, LINES, at_line, 0)

    def forward_halo():
        forward(2 - odd, 1, NEAR)
        forward(3 - 3 * odd, 1, FAR)

    boundary_sends(THEIRS)
    end_sends()
    boundary_sends(OWN)
    inner_sends(0)

    @pl.when(at_end)
    def _():
        inner_sends(1)

    fe[pl.ds(6 * odd, 2)] = jnp.zeros((2, 2, Y * R, R), F32)

    def side_copy(n):
        return pltpu.make_async_copy(side.at[n], halo_out.at[n], side_sem.at[n])

    @pl.when(tip)
    def _():
        side[...] = jnp.zeros_like(side)
        side_copy(0).start()
        side_copy(1).start()

    @pl.when(plain)
    def _():
        share(lambda rows: wait_for(recv_sem.at[THEIRS], 2, rows))
        forward(2 * odd, 2, AHEAD)
        inner_sends(1)
        share(lambda rows: wait_for(recv_sem.at[OWN], 2, rows))
        if FORWARD_STEP == 0:
            forward_halo()

    for copy in constants:
        copy.wait()

    def transform(groups):
        real = jnp.concatenate([re for re, _ in groups], axis=1)
        imag = jnp.concatenate([im for _, im in groups], axis=1)
        high, low = halves(jnp.concatenate([real, imag], axis=0))
        table = dft[...]
        section = dot(table, jnp.concatenate([high, high, low], axis=0))
        cos, sin = twist[0], twist[1]
        turned = []
        for n in range(len(groups)):
            re = section[:R, n * R : (n + 1) * R]
            im = section[R:, n * R : (n + 1) * R]
            turned.append(
                jnp.concatenate([re * cos - im * sin, re * sin + im * cos], axis=1)
            )
        high, low = halves(jnp.concatenate(turned, axis=0))
        final = dot_nt(table, jnp.concatenate([high, high, low], axis=1))
        return [
            (final[:R, n * R : (n + 1) * R], final[R:, n * R : (n + 1) * R])
            for n in range(len(groups))
        ]

    def series(slot, y):
        return tuple(rx[c, slot, pl.ds(y, R, stride=Y), :] for c in range(2))

    def plane_of(y):
        return pl.ds(pl.multiple_of(y * R, R), R)

    def own_pair(slot, where, p):
        groups_e, groups_n = [], []
        for n in range(2):
            y = 2 * p + n
            re, im = series(slot, y)
            intensity = re * re + im * im
            rate = ion_ref[y, 4 * me + where - 2] * jnp.exp(
                -BARRIER * lax.rsqrt(intensity + 1.0)
            )
            sums = dot(jnp.concatenate(halves(rate), axis=1), within[...])
            earlier = dot(before[...], jnp.concatenate(halves(sums[:, R:]), axis=0))
            plasma = 1.0 - jnp.exp(-(sums[:, :R] + earlier))
            groups_e.append((re, im))
            kerr = KERR * intensity
            groups_n.append((-kerr * im - plasma * re, kerr * re - plasma * im))
        spectra = transform(groups_e + groups_n)
        c = coupling[...]
        for n in range(2):
            at = plane_of(2 * p + n)
            e_re, e_im = spectra[n]
            n_re, n_im = spectra[2 + n]
            fe[where, 0, at, :] = e_re
            fe[where, 1, at, :] = e_im
            part[where - 2, 0, at, :] = e_re - c * n_im
            part[where - 2, 1, at, :] = e_im + c * n_re

    def halo_four(slot, where, p):
        spectra = transform([series(slot, 4 * p + y) for y in range(4)])
        for y in range(4):
            at = plane_of(4 * p + y)
            side[where, 0, at, :], side[where, 1, at, :] = spectra[y]

    def swap(i):
        where = 4 + i - 2 * odd
        return pltpu.make_async_remote_copy(
            src_ref=fe.at[where],
            dst_ref=fe.at[jnp.where(odd == 0, i, 6 + i)],
            send_sem=swap_send.at[i],
            recv_sem=swap_recv.at[i],
            device_id=(me + 1 - 2 * odd, g),
            device_id_type=MESH,
        )

    def spectrum_to_partner(n):
        return pltpu.make_async_remote_copy(
            src_ref=fe.at[jnp.where(odd == 0, 2 + n, 5 - n)],
            dst_ref=halo_out.at[n],
            send_sem=halo_send.at[n],
            recv_sem=halo_recv.at[n],
            device_id=(partner, partner_gx),
            device_id_type=MESH,
        )

    start = jnp.where(at_end, 0, BOUNDARY_STEP)

    def own_row(step, carry):
        @pl.when(jnp.logical_and(step == start, plain))
        def _():
            share(lambda rows: wait_for(recv_sem.at[AHEAD], 2, rows), of_partner=True)

        @pl.when(jnp.logical_and(step == start, at_end))
        def _():
            wait_for(recv_sem.at[OWN], 2, 1024)

        boundary = jnp.logical_and(step >= start, step < start + 2)
        i = jnp.where(boundary, step - start, jnp.where(step < start, step, step - 2))
        for n in range(2):

            @pl.when(jnp.logical_and(jnp.logical_not(boundary), i == n))
            def _(n=n):
                wait_for(recv_sem.at[INNER + n], 1, 1024)

        @pl.when(jnp.logical_and(step == FORWARD_STEP - 1, plain))
        def _():
            forward_halo()

        near_first = jnp.where(odd == 0, 2 + i, 1 - i)
        slot = jnp.where(boundary, near_first, 4 + i)
        where = jnp.where(boundary, near_first + 4 * odd, 4 + i - 2 * odd)

        def body(p, carry):
            own_pair(slot, where, p)
            return carry

        lax.fori_loop(0, Y // 2, body, 0, unroll=4)
        for n in range(2):

            @pl.when(jnp.logical_and(jnp.logical_not(boundary), i == n))
            def _(n=n):
                swap(n).start()

            @pl.when(jnp.logical_and(spectral, step == n))
            def _(n=n):
                spectrum_to_partner(n).start()

        return carry

    lax.fori_loop(0, ROWS, own_row, 0)

    def inner_terms(row):
        def block(n, carry):
            k = pl.multiple_of(n * 8, 8)
            d = diffraction[pl.ds(k, 8), :] * (1.0 / 12.0)
            lap = []
            for c in range(2):
                mid = [fe[row + 2, c, pl.ds(y * R + k, 8), :] for y in range(Y)]
                planes = []
                for y in range(Y):
                    at = pl.ds(y * R + k, 8)
                    near = fe[row + 1, c, at, :] + fe[row + 3, c, at, :]
                    far = fe[row, c, at, :] + fe[row + 4, c, at, :]
                    for o in (-1, 1):
                        if 0 <= y + o < Y:
                            near = near + mid[y + o]
                    for o in (-2, 2):
                        if 0 <= y + o < Y:
                            far = far + mid[y + o]
                    planes.append(16.0 * near - far - 60.0 * mid[y])
                lap.append(planes)
            for y in range(Y):
                at = pl.ds(y * R + k, 8)
                to = pl.ds(k * Y + y, 8, stride=Y)
                result[row, 0, to, :] = part[row, 0, at, :] - d * lap[1][y]
                result[row, 1, to, :] = part[row, 1, at, :] + d * lap[0][y]
            return carry

        lax.fori_loop(0, R // 8, block, 0)
        pltpu.make_async_copy(result.at[row], q_out.at[:, row], out_sem.at[row]).start()

    def terms_step(step, carry):
        @pl.when(step == 2)
        def _():
            for n in range(2):
                swap(n).wait_recv()

        inner_terms(jnp.where(odd == 0, step, ROWS - 1 - step))
        return carry

    lax.fori_loop(0, ROWS, terms_step, 0)

    def halo_step(n, carry):
        for i, kind in enumerate((NEAR, FAR)):

            @pl.when(n == i)
            def _(kind=kind):
                share(lambda rows: wait_for(recv_sem.at[kind], 1, rows), of_partner=True)

        slot = jnp.where(odd == 0, 1 - n, 2 + n)

        def body(p, carry):
            halo_four(slot, n, p)
            return carry

        lax.fori_loop(0, Y // 4, body, 0, unroll=2)
        side_copy(n).start()
        return carry

    @pl.when(plain)
    def _():
        lax.fori_loop(0, 2, halo_step, 0)

    for row in range(ROWS):
        pltpu.make_async_copy(result.at[row], q_out.at[:, row], out_sem.at[row]).wait()
    for n in range(2):
        swap(n).wait_send()
        wait_for(send_sem.at[INNER + n], 1, 31 * 32)
    wait_for(send_sem.at[OWN], 2, 19 * 32)

    @pl.when(plain)
    def _():
        wait_for(send_sem.at[THEIRS], 2, 11 * 32)
        share(lambda rows: wait_for(send_sem.at[AHEAD], 2, rows))
        share(lambda rows: wait_for(send_sem.at[NEAR], 1, rows))
        share(lambda rows: wait_for(send_sem.at[FAR], 1, rows))

    @pl.when(at_end)
    def _():
        wait_for(send_sem.at[THEIRS], 2, 12 * 32)

    @pl.when(spectral)
    def _():
        for n in range(2):
            spectrum_to_partner(n).wait()

    @pl.when(jnp.logical_or(plain, tip))
    def _():
        for n in range(2):
            side_copy(n).wait()


def add_halo(
    q_in, halo_in, diffraction_in, out,
    q, halo, diffraction, result, staged, q_sem, halo_sem, d_sem, out_sem, copy_sem,
):
    odd = lax.rem(lax.axis_index("ta"), 2)
    base = 2 * odd
    depth = R // PIECES

    def copies(n):
        wide = pl.ds(n * depth * Y, depth * Y)
        thin = pl.ds(n * depth, depth)
        rows = pl.ds(base, 2)
        return (
            pltpu.make_async_copy(q_in.at[:, rows, wide], q.at[:, :, wide], q_sem.at[n]),
            pltpu.make_async_copy(
                halo_in.at[:, :, :, thin], halo.at[:, :, :, thin], halo_sem.at[n]
            ),
            pltpu.make_async_copy(result.at[:, :, wide], out.at[:, rows, wide], out_sem.at[n]),
        )

    first = pltpu.make_async_copy(diffraction_in, diffraction, d_sem)
    first.start()
    for n in range(PIECES):
        for copy in copies(n)[:2]:
            copy.start()
    others = pl.ds(2 - base, 2)
    same_in = pltpu.make_async_copy(q_in.at[:, others], staged, copy_sem.at[0])
    same_out = pltpu.make_async_copy(staged, out.at[:, others], copy_sem.at[1])
    same_in.start()
    first.wait()
    for n in range(PIECES):
        for copy in copies(n)[:2]:
            copy.wait()

        def block(i, carry, n=n):
            k = pl.multiple_of(n * depth + 8 * i, 8)
            at_k = pl.ds(k, 8)
            d = diffraction[at_k, :] * (1.0 / 12.0)
            for y in range(Y):
                outer, second = [], []
                for c in range(2):
                    near, far = halo[0, c, y, at_k, :], halo[1, c, y, at_k, :]
                    outer.append(16.0 * near - far)
                    second.append(-near)
                at = pl.ds(k * Y + y, 8, stride=Y)
                for row, lap in ((odd, outer), (1 - odd, second)):
                    result[0, row, at, :] = q[0, row, at, :] - d * lap[1]
                    result[1, row, at, :] = q[1, row, at, :] + d * lap[0]
            return carry

        lax.fori_loop(0, depth // 8, block, 0)
        copies(n)[2].start()
        if n == COPY_AFTER:
            same_in.wait()
            same_out.start()
    same_out.wait()
    for n in range(PIECES):
        copies(n)[2].wait()


def on_device(field, ion_rate, diffraction, coupling):
    x_rows = field.shape[1]
    tiles = field.reshape(2, x_rows, Y, 4, R).transpose(0, 1, 3, 2, 4).reshape(2, x_rows, 32, R)
    dft, twist, within, before = tables()
    hbm = pl.BlockSpec(memory_space=pl.ANY)
    q, halo = pl.pallas_call(
        kernel,
        out_shape=[
            jax.ShapeDtypeStruct((2, ROWS, R * Y, R), F32),
            jax.ShapeDtypeStruct((2, 2, Y * R, R), F32),
        ],
        in_specs=[hbm] * 8,
        out_specs=[hbm, hbm],
        scratch_shapes=[
            pltpu.VMEM((2, ROWS + 2, R * Y, R), F32),
            pltpu.VMEM((ROWS + 4, 2, Y * R, R), F32),
            pltpu.VMEM((ROWS, 2, Y * R, R), F32),
            pltpu.VMEM((ROWS, 2, R * Y, R), F32),
            pltpu.VMEM((2, 2, Y * R, R), F32),
            pltpu.SMEM((Y, x_rows), F32),
            pltpu.VMEM((R, R), F32),
            pltpu.VMEM((R, R), F32),
            pltpu.VMEM(dft.shape, BF16),
            pltpu.VMEM(twist.shape, F32),
            pltpu.VMEM(within.shape, BF16),
            pltpu.VMEM(before.shape, BF16),
            pltpu.SemaphoreType.DMA((7,)),
            pltpu.SemaphoreType.DMA((7,)),
            pltpu.SemaphoreType.DMA((7,)),
            pltpu.SemaphoreType.DMA((2,)),
            pltpu.SemaphoreType.DMA((2,)),
            pltpu.SemaphoreType.DMA((2,)),
            pltpu.SemaphoreType.DMA((2,)),
            pltpu.SemaphoreType.DMA((2,)),
            pltpu.SemaphoreType.DMA((ROWS,)),
        ],
        compiler_params=pltpu.CompilerParams(
            collective_id=0, has_side_effects=True, vmem_limit_bytes=60 * 1024 * 1024
        ),
    )(
        ion_rate.T,
        tiles,
        coupling.reshape(R, R),
        diffraction.reshape(R, R),
        jnp.asarray(dft),
        jnp.asarray(twist),
        jnp.asarray(within),
        jnp.asarray(before),
    )
    spectrum = pl.pallas_call(
        add_halo,
        out_shape=jax.ShapeDtypeStruct((2, ROWS, R * Y, R), F32),
        in_specs=[hbm] * 3,
        out_specs=hbm,
        scratch_shapes=[
            pltpu.VMEM((2, 2, R * Y, R), F32),
            pltpu.VMEM((2, 2, Y, R, R), F32),
            pltpu.VMEM((R, R), F32),
            pltpu.VMEM((2, 2, R * Y, R), F32),
            pltpu.VMEM((2, 2, R * Y, R), F32),
            pltpu.SemaphoreType.DMA((PIECES,)),
            pltpu.SemaphoreType.DMA((PIECES,)),
            pltpu.SemaphoreType.DMA,
            pltpu.SemaphoreType.DMA((PIECES,)),
            pltpu.SemaphoreType.DMA((2,)),
        ],
        compiler_params=pltpu.CompilerParams(vmem_limit_bytes=60 * 1024 * 1024),
    )(q, halo.reshape(2, 2, Y, R, R), diffraction.reshape(R, R))
    spectrum = spectrum.reshape(2, ROWS, R, Y, R).transpose(0, 1, 3, 2, 4)
    return spectrum.reshape(2, ROWS, Y, R * R)


def solution(mesh):
    in_specs = (P(None, "gx", None, "ta"), P("gx", None), P(), P())
    out_specs = P(None, ("gx", "ta"), None, None)
    return jax.shard_map(
        on_device, mesh=mesh, in_specs=in_specs, out_specs=out_specs, check_vma=False
    )
```

```python
import functools
import math

import jax
import jax.numpy as jnp
import ml_dtypes
import numpy as np
from jax import lax
from jax.experimental import pallas as pl
from jax.experimental.pallas import tpu as pltpu
from jax.sharding import PartitionSpec as P

BARRIER = 2.0
KERR = 0.5
MESH = pl.DeviceIdType.MESH
R = 128
TA = 32
GX = 4
ROWS = 4
Y = 8
LINES = 4
COLS = 4
INNER, THEIRS, OWN, AHEAD, NEAR, FAR = 0, 2, 3, 4, 5, 6
BOUNDARY_STEP = 1
FORWARD_STEP = 2
DETOUR = (0,)
COPY_AFTER = 1
PIECES = 2
F32 = jnp.float32
BF16 = jnp.bfloat16


def tables():
    index = np.arange(R)
    angle = 2.0 * np.pi / R * (np.outer(index, index) % R)
    cos, sin = np.cos(angle), np.sin(angle)
    full = np.block([[cos, sin], [-sin, cos]]).astype(np.float32)
    high = full.astype(ml_dtypes.bfloat16)
    low = (full - high.astype(np.float32)).astype(ml_dtypes.bfloat16)
    dft = np.concatenate([high, low, high], axis=1)
    turn = 2.0 * np.pi / (R * R) * np.outer(index, index)
    twist = np.stack([np.cos(turn), -np.sin(turn)]) / R
    upper = (index[:, None] <= index[None, :]).astype(np.float32)
    within = np.concatenate([upper, np.ones((R, R), np.float32)], axis=1)
    within = np.concatenate([within, within], axis=0)
    lower = (index[:, None] > index[None, :]).astype(np.float32)
    before = np.concatenate([lower, lower], axis=1)
    return (
        dft,
        twist.astype(np.float32),
        within.astype(ml_dtypes.bfloat16),
        before.astype(ml_dtypes.bfloat16),
    )


def detours(lines):
    return functools.reduce(jnp.logical_or, [lines == n for n in DETOUR])


def halves(v):
    high = v.astype(BF16)
    return high, (v - high.astype(F32)).astype(BF16)


def dot(a, b):
    return jnp.dot(a, b, preferred_element_type=F32)


def dot_nt(a, b):
    return lax.dot_general(a, b, (((1,), (1,)), ((), ())), preferred_element_type=F32)


def kernel(
    ion_in, field, coupling_in, diffraction_in, dft_in, twist_in, within_in, before_in,
    q_out, halo_out,
    rx, fe, part, result, side, ion_ref, coupling, diffraction, dft, twist, within, before,
    const_sem, send_sem, recv_sem, swap_send, swap_recv, halo_send, halo_recv, side_sem, out_sem,
):
    me = lax.axis_index("ta")
    g = lax.axis_index("gx")
    odd = lax.rem(me, 2)
    away = 1 - 2 * odd
    chip = me // 2
    col = lax.rem(chip, COLS)
    line = chip // COLS
    first, last = me == 0, me == TA - 1
    at_end = jnp.logical_or(lax.rem(me, 8) == 0, lax.rem(me, 8) == 7)
    plain = jnp.logical_not(at_end)
    tip = jnp.logical_or(jnp.logical_and(first, g == 0), jnp.logical_and(last, g == GX - 1))
    paired = jnp.logical_not(tip)
    cross = jnp.logical_and(paired, jnp.logical_or(first, last))
    spectral = jnp.logical_and(paired, at_end)
    wide = jnp.logical_or(
        jnp.logical_and(odd == 0, col == 1), jnp.logical_and(odd == 1, col == COLS - 2)
    )
    thin = jnp.logical_or(
        jnp.logical_and(odd == 1, col == 0), jnp.logical_and(odd == 0, col == COLS - 1)
    )
    even_share = jnp.logical_and(plain, jnp.logical_not(jnp.logical_or(wide, thin)))
    partner = lax.rem(me + TA - away, TA)
    partner_gx = jnp.where(first, lax.rem(g + GX - 1, GX), jnp.where(last, lax.rem(g + 1, GX), g))

    gate = pltpu.get_barrier_semaphore()

    def greet(off, carry):
        pl.semaphore_signal(
            gate, inc=1, device_id=(lax.rem(me + off, TA), g), device_id_type=MESH
        )
        return carry

    lax.fori_loop(1, TA, greet, 0)

    @pl.when(cross)
    def _():
        pl.semaphore_signal(gate, inc=1, device_id=(partner, partner_gx), device_id_type=MESH)

    pl.semaphore_wait(gate, TA - 1 + jnp.where(cross, 1, 0))

    constants = [
        pltpu.make_async_copy(src, dst, const_sem.at[n])
        for n, (src, dst) in enumerate(
            [
                (ion_in, ion_ref),
                (coupling_in, coupling),
                (diffraction_in, diffraction),
                (dft_in, dft),
                (twist_in, twist),
                (within_in, within),
                (before_in, before),
            ]
        )
    ]
    for copy in constants:
        copy.start()

    place = pl.ds(pl.multiple_of(me * 32, 32), 32)

    def send(to, row, slot, count, kind):
        pltpu.make_async_remote_copy(
            src_ref=field.at[:, pl.ds(row, count)],
            dst_ref=rx.at[:, pl.ds(slot, count), place],
            send_sem=send_sem.at[kind],
            recv_sem=recv_sem.at[kind],
            device_id=(to, g),
            device_id_type=MESH,
        ).start()

    def keep(row, slot, count, kind):
        pltpu.make_async_copy(
            field.at[:, pl.ds(row, count)],
            rx.at[:, pl.ds(slot, count), place],
            recv_sem.at[kind],
        ).start()

    def deliver(act, core, kind, to):
        if kind == OWN:
            act(4 * to + 2 * core, 2 - 2 * core, 2, OWN)
        else:
            act(4 * to - 2 + 6 * core, 2 * core, 2, THEIRS)

    def boundary_sends(kind):
        def at_line(j, carry):
            y = lax.rem(line + j, LINES)
            detour = detours(lax.rem(LINES - j, LINES))
            for shift, core in ((2, 0), (2, 1), (3, 0), (1, 1), (0, 0), (0, 1)):
                column = lax.rem(col + shift, COLS)
                to = 8 * y + 2 * column + core
                fits = column != (0 if core == 0 else COLS - 1)
                if shift == 2:
                    fits = jnp.logical_and(col == (COLS - 1 if core == 0 else 0), detour)
                if shift in (1, 3):
                    far = column == (COLS - 1 if core == 0 else 0)
                    fits = jnp.logical_and(fits, jnp.logical_not(jnp.logical_and(far, detour)))
                if shift == 0:
                    fits = jnp.logical_and(fits, to != me)

                @pl.when(fits)
                def _(to=to, core=core):
                    deliver(functools.partial(send, to), core, kind, to)

            return carry

        lax.fori_loop(0, LINES, at_line, 0)
        for core in range(2):

            @pl.when(jnp.logical_and(plain, odd == core))
            def _(core=core):
                deliver(keep, core, kind, me)

    def end_sends():
        def at_line(j, carry):
            y = lax.rem(line + j, LINES)
            for to, core in ((8 * y, 0), (8 * y + 7, 1)):

                @pl.when(to != me)
                def _(to=to, core=core):
                    deliver(functools.partial(send, to), core, OWN, to)

            return carry

        lax.fori_loop(0, LINES, at_line, 0)
        for core in range(2):

            @pl.when(jnp.logical_and(at_end, odd == core))
            def _(core=core):
                deliver(keep, core, OWN, me)

    def inner_sends(i):
        def send_inner(off, carry):
            to = lax.rem(me + off, TA)
            send(to, 4 * to + 2 * (1 - lax.rem(to, 2)) + i, 4 + i, 1, INNER + i)
            return carry

        lax.fori_loop(1, TA, send_inner, 0)
        keep(4 * me + 2 * (1 - odd) + i, 4 + i, 1, INNER + i)

    def wait_for(sem, slots, rows):
        ref = rx.at[:, pl.ds(0, slots), pl.ds(0, rows)]
        pltpu.make_async_copy(ref, ref, sem).wait()

    def share(action, of_partner=False):
        more, less = 512 + 64 * len(DETOUR), 512 - 64 * len(DETOUR)
        for when, rows in (
            (even_share, 512),
            (thin if of_partner else wide, more),
            (wide if of_partner else thin, less),
        ):

            @pl.when(when)
            def _(rows=rows):
                action(rows)

    def forward(slot, count, kind):
        def one(column, y):
            at = pl.ds(pl.multiple_of(256 * y + 64 * column, 64), 64)
            pltpu.make_async_remote_copy(
                src_ref=rx.at[:, pl.ds(slot, count), at],
                dst_ref=rx.at[:, pl.ds(slot, count), at],
                send_sem=send_sem.at[kind],
                recv_sem=recv_sem.at[kind],
                device_id=(partner, partner_gx),
                device_id_type=MESH,
            ).start()

        def at_line(y, carry):
            detour = detours(lax.rem(y - line + LINES, LINES))
            one(col, y)

            @pl.when(jnp.logical_not(jnp.logical_and(thin, detour)))
            def _():
                one(lax.rem(col + jnp.where(odd == 0, 1, 3), COLS), y)

            @pl.when(jnp.logical_and(wide, detour))
            def _():
                one(lax.rem(col + 2, COLS), y)

            return carry

        lax.fori_loop(0, LINES, at_line, 0)

    def forward_halo():
        forward(2 - odd, 1, NEAR)
        forward(3 - 3 * odd, 1, FAR)

    end_sends()
    boundary_sends(THEIRS)
    boundary_sends(OWN)
    inner_sends(0)

    @pl.when(at_end)
    def _():
        inner_sends(1)

    fe[pl.ds(6 * odd, 2)] = jnp.zeros((2, 2, Y * R, R), F32)

    def side_copy(n):
        return pltpu.make_async_copy(side.at[n], halo_out.at[n], side_sem.at[n])

    @pl.when(tip)
    def _():
        side[...] = jnp.zeros_like(side)
        side_copy(0).start()
        side_copy(1).start()

    @pl.when(plain)
    def _():
        share(lambda rows: wait_for(recv_sem.at[THEIRS], 2, rows))
        forward(2 * odd, 2, AHEAD)
        inner_sends(1)
        share(lambda rows: wait_for(recv_sem.at[OWN], 2, rows))
        if FORWARD_STEP == 0:
            forward_halo()

    for copy in constants:
        copy.wait()

    def transform(groups):
        real = jnp.concatenate([re for re, _ in groups], axis=1)
        imag = jnp.concatenate([im for _, im in groups], axis=1)
        high, low = halves(jnp.concatenate([real, imag], axis=0))
        table = dft[...]
        section = dot(table, jnp.concatenate([high, high, low], axis=0))
        cos, sin = twist[0], twist[1]
        turned = []
        for n in range(len(groups)):
            re = section[:R, n * R : (n + 1) * R]
            im = section[R:, n * R : (n + 1) * R]
            turned.append(
                jnp.concatenate([re * cos - im * sin, re * sin + im * cos], axis=1)
            )
        high, low = halves(jnp.concatenate(turned, axis=0))
        final = dot_nt(table, jnp.concatenate([high, high, low], axis=1))
        return [
            (final[:R, n * R : (n + 1) * R], final[R:, n * R : (n + 1) * R])
            for n in range(len(groups))
        ]

    def series(slot, y):
        return tuple(rx[c, slot, pl.ds(y, R, stride=Y), :] for c in range(2))

    def plane_of(y):
        return pl.ds(pl.multiple_of(y * R, R), R)

    def own_pair(slot, where, p):
        groups_e, groups_n = [], []
        for n in range(2):
            y = 2 * p + n
            re, im = series(slot, y)
            intensity = re * re + im * im
            rate = ion_ref[y, 4 * me + where - 2] * jnp.exp(
                -BARRIER * lax.rsqrt(intensity + 1.0)
            )
            sums = dot(jnp.concatenate(halves(rate), axis=1), within[...])
            earlier = dot(before[...], jnp.concatenate(halves(sums[:, R:]), axis=0))
            plasma = 1.0 - jnp.exp(-(sums[:, :R] + earlier))
            groups_e.append((re, im))
            kerr = KERR * intensity
            groups_n.append((-kerr * im - plasma * re, kerr * re - plasma * im))
        spectra = transform(groups_e + groups_n)
        c = coupling[...]
        for n in range(2):
            at = plane_of(2 * p + n)
            e_re, e_im = spectra[n]
            n_re, n_im = spectra[2 + n]
            fe[where, 0, at, :] = e_re
            fe[where, 1, at, :] = e_im
            part[where - 2, 0, at, :] = e_re - c * n_im
            part[where - 2, 1, at, :] = e_im + c * n_re

    def halo_four(slot, where, p):
        spectra = transform([series(slot, 4 * p + y) for y in range(4)])
        for y in range(4):
            at = plane_of(4 * p + y)
            side[where, 0, at, :], side[where, 1, at, :] = spectra[y]

    def swap(i):
        where = 4 + i - 2 * odd
        return pltpu.make_async_remote_copy(
            src_ref=fe.at[where],
            dst_ref=fe.at[jnp.where(odd == 0, i, 6 + i)],
            send_sem=swap_send.at[i],
            recv_sem=swap_recv.at[i],
            device_id=(me + 1 - 2 * odd, g),
            device_id_type=MESH,
        )

    def spectrum_to_partner(n):
        return pltpu.make_async_remote_copy(
            src_ref=fe.at[jnp.where(odd == 0, 2 + n, 5 - n)],
            dst_ref=halo_out.at[n],
            send_sem=halo_send.at[n],
            recv_sem=halo_recv.at[n],
            device_id=(partner, partner_gx),
            device_id_type=MESH,
        )

    start = jnp.where(at_end, 0, BOUNDARY_STEP)

    def own_row(step, carry):
        @pl.when(jnp.logical_and(step == start, plain))
        def _():
            share(lambda rows: wait_for(recv_sem.at[AHEAD], 2, rows), of_partner=True)

        @pl.when(jnp.logical_and(step == start, at_end))
        def _():
            wait_for(recv_sem.at[OWN], 2, 1024)

        boundary = jnp.logical_and(step >= start, step < start + 2)
        i = jnp.where(boundary, step - start, jnp.where(step < start, step, step - 2))
        for n in range(2):

            @pl.when(jnp.logical_and(jnp.logical_not(boundary), i == n))
            def _(n=n):
                wait_for(recv_sem.at[INNER + n], 1, 1024)

        @pl.when(jnp.logical_and(step == FORWARD_STEP - 1, plain))
        def _():
            forward_halo()

        near_first = jnp.where(odd == 0, 2 + i, 1 - i)
        slot = jnp.where(boundary, near_first, 4 + i)
        where = jnp.where(boundary, near_first + 4 * odd, 4 + i - 2 * odd)

        def body(p, carry):
            own_pair(slot, where, p)
            return carry

        lax.fori_loop(0, Y // 2, body, 0, unroll=4)
        for n in range(2):

            @pl.when(jnp.logical_and(jnp.logical_not(boundary), i == n))
            def _(n=n):
                swap(n).start()

            @pl.when(jnp.logical_and(spectral, step == n))
            def _(n=n):
                spectrum_to_partner(n).start()

        return carry

    lax.fori_loop(0, ROWS, own_row, 0)

    def inner_terms(row):
        def block(n, carry):
            k = pl.multiple_of(n * 8, 8)
            d = diffraction[pl.ds(k, 8), :] * (1.0 / 12.0)
            lap = []
            for c in range(2):
                mid = [fe[row + 2, c, pl.ds(y * R + k, 8), :] for y in range(Y)]
                planes = []
                for y in range(Y):
                    at = pl.ds(y * R + k, 8)
                    near = fe[row + 1, c, at, :] + fe[row + 3, c, at, :]
                    far = fe[row, c, at, :] + fe[row + 4, c, at, :]
                    for o in (-1, 1):
                        if 0 <= y + o < Y:
                            near = near + mid[y + o]
                    for o in (-2, 2):
                        if 0 <= y + o < Y:
                            far = far + mid[y + o]
                    planes.append(16.0 * near - far - 60.0 * mid[y])
                lap.append(planes)
            for y in range(Y):
                at = pl.ds(y * R + k, 8)
                to = pl.ds(k * Y + y, 8, stride=Y)
                result[row, 0, to, :] = part[row, 0, at, :] - d * lap[1][y]
                result[row, 1, to, :] = part[row, 1, at, :] + d * lap[0][y]
            return carry

        lax.fori_loop(0, R // 8, block, 0)
        pltpu.make_async_copy(result.at[row], q_out.at[:, row], out_sem.at[row]).start()

    def terms_step(step, carry):
        @pl.when(step == 2)
        def _():
            for n in range(2):
                swap(n).wait_recv()

        inner_terms(jnp.where(odd == 0, step, ROWS - 1 - step))
        return carry

    lax.fori_loop(0, ROWS, terms_step, 0)

    def halo_step(n, carry):
        for i, kind in enumerate((NEAR, FAR)):

            @pl.when(n == i)
            def _(kind=kind):
                share(lambda rows: wait_for(recv_sem.at[kind], 1, rows), of_partner=True)

        slot = jnp.where(odd == 0, 1 - n, 2 + n)

        def body(p, carry):
            halo_four(slot, n, p)
            return carry

        lax.fori_loop(0, Y // 4, body, 0, unroll=2)
        side_copy(n).start()
        return carry

    @pl.when(plain)
    def _():
        lax.fori_loop(0, 2, halo_step, 0)

    for row in range(ROWS):
        pltpu.make_async_copy(result.at[row], q_out.at[:, row], out_sem.at[row]).wait()
    for n in range(2):
        swap(n).wait_send()
        wait_for(send_sem.at[INNER + n], 1, 31 * 32)
    wait_for(send_sem.at[OWN], 2, 19 * 32)

    @pl.when(plain)
    def _():
        wait_for(send_sem.at[THEIRS], 2, 11 * 32)
        share(lambda rows: wait_for(send_sem.at[AHEAD], 2, rows))
        share(lambda rows: wait_for(send_sem.at[NEAR], 1, rows))
        share(lambda rows: wait_for(send_sem.at[FAR], 1, rows))

    @pl.when(at_end)
    def _():
        wait_for(send_sem.at[THEIRS], 2, 12 * 32)

    @pl.when(spectral)
    def _():
        for n in range(2):
            spectrum_to_partner(n).wait()

    @pl.when(jnp.logical_or(plain, tip))
    def _():
        for n in range(2):
            side_copy(n).wait()


def add_halo(
    q_in, halo_in, diffraction_in, out,
    q, halo, diffraction, result, staged, q_sem, halo_sem, d_sem, out_sem, copy_sem,
):
    odd = lax.rem(lax.axis_index("ta"), 2)
    base = 2 * odd
    depth = R // PIECES

    def copies(n):
        wide = pl.ds(n * depth * Y, depth * Y)
        thin = pl.ds(n * depth, depth)
        rows = pl.ds(base, 2)
        return (
            pltpu.make_async_copy(q_in.at[:, rows, wide], q.at[:, :, wide], q_sem.at[n]),
            pltpu.make_async_copy(
                halo_in.at[:, :, :, thin], halo.at[:, :, :, thin], halo_sem.at[n]
            ),
            pltpu.make_async_copy(result.at[:, :, wide], out.at[:, rows, wide], out_sem.at[n]),
        )

    first = pltpu.make_async_copy(diffraction_in, diffraction, d_sem)
    first.start()
    for n in range(PIECES):
        for copy in copies(n)[:2]:
            copy.start()
    others = pl.ds(2 - base, 2)
    same_in = pltpu.make_async_copy(q_in.at[:, others], staged, copy_sem.at[0])
    same_out = pltpu.make_async_copy(staged, out.at[:, others], copy_sem.at[1])
    same_in.start()
    first.wait()
    for n in range(PIECES):
        for copy in copies(n)[:2]:
            copy.wait()

        def block(i, carry, n=n):
            k = pl.multiple_of(n * depth + 8 * i, 8)
            at_k = pl.ds(k, 8)
            d = diffraction[at_k, :] * (1.0 / 12.0)
            for y in range(Y):
                outer, second = [], []
                for c in range(2):
                    near, far = halo[0, c, y, at_k, :], halo[1, c, y, at_k, :]
                    outer.append(16.0 * near - far)
                    second.append(-near)
                at = pl.ds(k * Y + y, 8, stride=Y)
                for row, lap in ((odd, outer), (1 - odd, second)):
                    result[0, row, at, :] = q[0, row, at, :] - d * lap[1]
                    result[1, row, at, :] = q[1, row, at, :] + d * lap[0]
            return carry

        lax.fori_loop(0, depth // 8, block, 0)
        copies(n)[2].start()
        if n == COPY_AFTER:
            same_in.wait()
            same_out.start()
    same_out.wait()
    for n in range(PIECES):
        copies(n)[2].wait()


def on_device(field, ion_rate, diffraction, coupling):
    x_rows = field.shape[1]
    tiles = field.reshape(2, x_rows, Y, 4, R).transpose(0, 1, 3, 2, 4).reshape(2, x_rows, 32, R)
    dft, twist, within, before = tables()
    hbm = pl.BlockSpec(memory_space=pl.ANY)
    q, halo = pl.pallas_call(
        kernel,
        out_shape=[
            jax.ShapeDtypeStruct((2, ROWS, R * Y, R), F32),
            jax.ShapeDtypeStruct((2, 2, Y * R, R), F32),
        ],
        in_specs=[hbm] * 8,
        out_specs=[hbm, hbm],
        scratch_shapes=[
            pltpu.VMEM((2, ROWS + 2, R * Y, R), F32),
            pltpu.VMEM((ROWS + 4, 2, Y * R, R), F32),
            pltpu.VMEM((ROWS, 2, Y * R, R), F32),
            pltpu.VMEM((ROWS, 2, R * Y, R), F32),
            pltpu.VMEM((2, 2, Y * R, R), F32),
            pltpu.SMEM((Y, x_rows), F32),
            pltpu.VMEM((R, R), F32),
            pltpu.VMEM((R, R), F32),
            pltpu.VMEM(dft.shape, BF16),
            pltpu.VMEM(twist.shape, F32),
            pltpu.VMEM(within.shape, BF16),
            pltpu.VMEM(before.shape, BF16),
            pltpu.SemaphoreType.DMA((7,)),
            pltpu.SemaphoreType.DMA((7,)),
            pltpu.SemaphoreType.DMA((7,)),
            pltpu.SemaphoreType.DMA((2,)),
            pltpu.SemaphoreType.DMA((2,)),
            pltpu.SemaphoreType.DMA((2,)),
            pltpu.SemaphoreType.DMA((2,)),
            pltpu.SemaphoreType.DMA((2,)),
            pltpu.SemaphoreType.DMA((ROWS,)),
        ],
        compiler_params=pltpu.CompilerParams(
            collective_id=0, has_side_effects=True, vmem_limit_bytes=60 * 1024 * 1024
        ),
    )(
        ion_rate.T,
        tiles,
        coupling.reshape(R, R),
        diffraction.reshape(R, R),
        jnp.asarray(dft),
        jnp.asarray(twist),
        jnp.asarray(within),
        jnp.asarray(before),
    )
    spectrum = pl.pallas_call(
        add_halo,
        out_shape=jax.ShapeDtypeStruct((2, ROWS, R * Y, R), F32),
        in_specs=[hbm] * 3,
        out_specs=hbm,
        scratch_shapes=[
            pltpu.VMEM((2, 2, R * Y, R), F32),
            pltpu.VMEM((2, 2, Y, R, R), F32),
            pltpu.VMEM((R, R), F32),
            pltpu.VMEM((2, 2, R * Y, R), F32),
            pltpu.VMEM((2, 2, R * Y, R), F32),
            pltpu.SemaphoreType.DMA((PIECES,)),
            pltpu.SemaphoreType.DMA((PIECES,)),
            pltpu.SemaphoreType.DMA,
            pltpu.SemaphoreType.DMA((PIECES,)),
            pltpu.SemaphoreType.DMA((2,)),
        ],
        compiler_params=pltpu.CompilerParams(vmem_limit_bytes=60 * 1024 * 1024),
    )(q, halo.reshape(2, 2, Y, R, R), diffraction.reshape(R, R))
    spectrum = spectrum.reshape(2, ROWS, R, Y, R).transpose(0, 1, 3, 2, 4)
    return spectrum.reshape(2, ROWS, Y, R * R)


def solution(mesh):
    in_specs = (P(None, "gx", None, "ta"), P("gx", None), P(), P())
    out_specs = P(None, ("gx", "ta"), None, None)
    return jax.shard_map(
        on_device, mesh=mesh, in_specs=in_specs, out_specs=out_specs, check_vma=False
    )
```

```python
import functools
import math

import jax
import jax.numpy as jnp
import ml_dtypes
import numpy as np
from jax import lax
from jax.experimental import pallas as pl
from jax.experimental.pallas import tpu as pltpu
from jax.sharding import PartitionSpec as P

BARRIER = 2.0
KERR = 0.5
MESH = pl.DeviceIdType.MESH
R = 128
TA = 32
GX = 4
ROWS = 4
Y = 8
LINES = 4
COLS = 4
INNER, THEIRS, OWN, AHEAD, NEAR, FAR = 0, 2, 3, 4, 5, 6
BOUNDARY_STEP = 1
FORWARD_STEP = 0
DETOUR = (0,)
COPY_AFTER = 0
PIECES = 2
F32 = jnp.float32
BF16 = jnp.bfloat16


def tables():
    index = np.arange(R)
    angle = 2.0 * np.pi / R * (np.outer(index, index) % R)
    cos, sin = np.cos(angle), np.sin(angle)
    full = np.block([[cos, sin], [-sin, cos]]).astype(np.float32)
    high = full.astype(ml_dtypes.bfloat16)
    low = (full - high.astype(np.float32)).astype(ml_dtypes.bfloat16)
    dft = np.concatenate([high, low, high], axis=1)
    turn = 2.0 * np.pi / (R * R) * np.outer(index, index)
    twist = np.stack([np.cos(turn), -np.sin(turn)]) / R
    upper = (index[:, None] <= index[None, :]).astype(np.float32)
    within = np.concatenate([upper, np.ones((R, R), np.float32)], axis=1)
    within = np.concatenate([within, within], axis=0)
    lower = (index[:, None] > index[None, :]).astype(np.float32)
    before = np.concatenate([lower, lower], axis=1)
    return (
        dft,
        twist.astype(np.float32),
        within.astype(ml_dtypes.bfloat16),
        before.astype(ml_dtypes.bfloat16),
    )


def detours(lines):
    return functools.reduce(jnp.logical_or, [lines == n for n in DETOUR])


def halves(v):
    high = v.astype(BF16)
    return high, (v - high.astype(F32)).astype(BF16)


def dot(a, b):
    return jnp.dot(a, b, preferred_element_type=F32)


def dot_nt(a, b):
    return lax.dot_general(a, b, (((1,), (1,)), ((), ())), preferred_element_type=F32)


def kernel(
    ion_in, field, coupling_in, diffraction_in, dft_in, twist_in, within_in, before_in,
    q_out, halo_out,
    rx, fe, part, result, side, ion_ref, coupling, diffraction, dft, twist, within, before,
    const_sem, send_sem, recv_sem, swap_send, swap_recv, halo_send, halo_recv, side_sem, out_sem,
):
    me = lax.axis_index("ta")
    g = lax.axis_index("gx")
    odd = lax.rem(me, 2)
    away = 1 - 2 * odd
    chip = me // 2
    col = lax.rem(chip, COLS)
    line = chip // COLS
    first, last = me == 0, me == TA - 1
    at_end = jnp.logical_or(lax.rem(me, 8) == 0, lax.rem(me, 8) == 7)
    plain = jnp.logical_not(at_end)
    tip = jnp.logical_or(jnp.logical_and(first, g == 0), jnp.logical_and(last, g == GX - 1))
    paired = jnp.logical_not(tip)
    cross = jnp.logical_and(paired, jnp.logical_or(first, last))
    spectral = jnp.logical_and(paired, at_end)
    wide = jnp.logical_or(
        jnp.logical_and(odd == 0, col == 1), jnp.logical_and(odd == 1, col == COLS - 2)
    )
    thin = jnp.logical_or(
        jnp.logical_and(odd == 1, col == 0), jnp.logical_and(odd == 0, col == COLS - 1)
    )
    even_share = jnp.logical_and(plain, jnp.logical_not(jnp.logical_or(wide, thin)))
    partner = lax.rem(me + TA - away, TA)
    partner_gx = jnp.where(first, lax.rem(g + GX - 1, GX), jnp.where(last, lax.rem(g + 1, GX), g))

    gate = pltpu.get_barrier_semaphore()

    def greet(off, carry):
        pl.semaphore_signal(
            gate, inc=1, device_id=(lax.rem(me + off, TA), g), device_id_type=MESH
        )
        return carry

    lax.fori_loop(1, TA, greet, 0)

    @pl.when(cross)
    def _():
        pl.semaphore_signal(gate, inc=1, device_id=(partner, partner_gx), device_id_type=MESH)

    pl.semaphore_wait(gate, TA - 1 + jnp.where(cross, 1, 0))

    constants = [
        pltpu.make_async_copy(src, dst, const_sem.at[n])
        for n, (src, dst) in enumerate(
            [
                (ion_in, ion_ref),
                (coupling_in, coupling),
                (diffraction_in, diffraction),
                (dft_in, dft),
                (twist_in, twist),
                (within_in, within),
                (before_in, before),
            ]
        )
    ]
    for copy in constants:
        copy.start()

    place = pl.ds(pl.multiple_of(me * 32, 32), 32)

    def send(to, row, slot, count, kind):
        pltpu.make_async_remote_copy(
            src_ref=field.at[:, pl.ds(row, count)],
            dst_ref=rx.at[:, pl.ds(slot, count), place],
            send_sem=send_sem.at[kind],
            recv_sem=recv_sem.at[kind],
            device_id=(to, g),
            device_id_type=MESH,
        ).start()

    def keep(row, slot, count, kind):
        pltpu.make_async_copy(
            field.at[:, pl.ds(row, count)],
            rx.at[:, pl.ds(slot, count), place],
            recv_sem.at[kind],
        ).start()

    def deliver(act, core, kind, to):
        if kind == OWN:
            act(4 * to + 2 * core, 2 - 2 * core, 2, OWN)
        else:
            act(4 * to - 2 + 6 * core, 2 * core, 2, THEIRS)

    def boundary_sends(kind):
        def at_line(j, carry):
            y = lax.rem(line + j, LINES)
            detour = detours(lax.rem(LINES - j, LINES))
            for shift, core in ((2, 0), (2, 1), (3, 0), (1, 1), (0, 0), (0, 1)):
                column = lax.rem(col + shift, COLS)
                to = 8 * y + 2 * column + core
                fits = column != (0 if core == 0 else COLS - 1)
                if shift == 2:
                    fits = jnp.logical_and(col == (COLS - 1 if core == 0 else 0), detour)
                if shift in (1, 3):
                    far = column == (COLS - 1 if core == 0 else 0)
                    fits = jnp.logical_and(fits, jnp.logical_not(jnp.logical_and(far, detour)))
                if shift == 0:
                    fits = jnp.logical_and(fits, to != me)

                @pl.when(fits)
                def _(to=to, core=core):
                    deliver(functools.partial(send, to), core, kind, to)

            return carry

        lax.fori_loop(0, LINES, at_line, 0)
        for core in range(2):

            @pl.when(jnp.logical_and(plain, odd == core))
            def _(core=core):
                deliver(keep, core, kind, me)

    def end_sends():
        def at_line(j, carry):
            y = lax.rem(line + j, LINES)
            for to, core in ((8 * y, 0), (8 * y + 7, 1)):

                @pl.when(to != me)
                def _(to=to, core=core):
                    deliver(functools.partial(send, to), core, OWN, to)

            return carry

        lax.fori_loop(0, LINES, at_line, 0)
        for core in range(2):

            @pl.when(jnp.logical_and(at_end, odd == core))
            def _(core=core):
                deliver(keep, core, OWN, me)

    def inner_sends(i):
        def send_inner(off, carry):
            to = lax.rem(me + off, TA)
            send(to, 4 * to + 2 * (1 - lax.rem(to, 2)) + i, 4 + i, 1, INNER + i)
            return carry

        lax.fori_loop(1, TA, send_inner, 0)
        keep(4 * me + 2 * (1 - odd) + i, 4 + i, 1, INNER + i)

    def wait_for(sem, slots, rows):
        ref = rx.at[:, pl.ds(0, slots), pl.ds(0, rows)]
        pltpu.make_async_copy(ref, ref, sem).wait()

    def share(action, of_partner=False):
        more, less = 512 + 64 * len(DETOUR), 512 - 64 * len(DETOUR)
        for when, rows in (
            (even_share, 512),
            (thin if of_partner else wide, more),
            (wide if of_partner else thin, less),
        ):

            @pl.when(when)
            def _(rows=rows):
                action(rows)

    def forward(slot, count, kind):
        def one(column, y):
            at = pl.ds(pl.multiple_of(256 * y + 64 * column, 64), 64)
            pltpu.make_async_remote_copy(
                src_ref=rx.at[:, pl.ds(slot, count), at],
                dst_ref=rx.at[:, pl.ds(slot, count), at],
                send_sem=send_sem.at[kind],
                recv_sem=recv_sem.at[kind],
                device_id=(partner, partner_gx),
                device_id_type=MESH,
            ).start()

        def at_line(y, carry):
            detour = detours(lax.rem(y - line + LINES, LINES))
            one(col, y)

            @pl.when(jnp.logical_not(jnp.logical_and(thin, detour)))
            def _():
                one(lax.rem(col + jnp.where(odd == 0, 1, 3), COLS), y)

            @pl.when(jnp.logical_and(wide, detour))
            def _():
                one(lax.rem(col + 2, COLS), y)

            return carry

        lax.fori_loop(0, LINES, at_line, 0)

    def forward_halo():
        forward(2 - odd, 1, NEAR)
        forward(3 - 3 * odd, 1, FAR)

    end_sends()
    boundary_sends(THEIRS)
    boundary_sends(OWN)
    inner_sends(0)

    @pl.when(at_end)
    def _():
        inner_sends(1)

    fe[pl.ds(6 * odd, 2)] = jnp.zeros((2, 2, Y * R, R), F32)

    def side_copy(n):
        return pltpu.make_async_copy(side.at[n], halo_out.at[n], side_sem.at[n])

    @pl.when(tip)
    def _():
        side[...] = jnp.zeros_like(side)
        side_copy(0).start()
        side_copy(1).start()

    @pl.when(plain)
    def _():
        share(lambda rows: wait_for(recv_sem.at[THEIRS], 2, rows))
        forward(2 * odd, 2, AHEAD)
        inner_sends(1)
        share(lambda rows: wait_for(recv_sem.at[OWN], 2, rows))
        if FORWARD_STEP == 0:
            forward_halo()

    for copy in constants:
        copy.wait()

    def transform(groups):
        real = jnp.concatenate([re for re, _ in groups], axis=1)
        imag = jnp.concatenate([im for _, im in groups], axis=1)
        high, low = halves(jnp.concatenate([real, imag], axis=0))
        table = dft[...]
        section = dot(table, jnp.concatenate([high, high, low], axis=0))
        cos, sin = twist[0], twist[1]
        turned = []
        for n in range(len(groups)):
            re = section[:R, n * R : (n + 1) * R]
            im = section[R:, n * R : (n + 1) * R]
            turned.append(
                jnp.concatenate([re * cos - im * sin, re * sin + im * cos], axis=1)
            )
        high, low = halves(jnp.concatenate(turned, axis=0))
        final = dot_nt(table, jnp.concatenate([high, high, low], axis=1))
        return [
            (final[:R, n * R : (n + 1) * R], final[R:, n * R : (n + 1) * R])
            for n in range(len(groups))
        ]

    def series(slot, y):
        return tuple(rx[c, slot, pl.ds(y, R, stride=Y), :] for c in range(2))

    def plane_of(y):
        return pl.ds(pl.multiple_of(y * R, R), R)

    def own_pair(slot, where, p):
        groups_e, groups_n = [], []
        for n in range(2):
            y = 2 * p + n
            re, im = series(slot, y)
            intensity = re * re + im * im
            rate = ion_ref[y, 4 * me + where - 2] * jnp.exp(
                -BARRIER * lax.rsqrt(intensity + 1.0)
            )
            sums = dot(jnp.concatenate(halves(rate), axis=1), within[...])
            earlier = dot(before[...], jnp.concatenate(halves(sums[:, R:]), axis=0))
            plasma = 1.0 - jnp.exp(-(sums[:, :R] + earlier))
            groups_e.append((re, im))
            kerr = KERR * intensity
            groups_n.append((-kerr * im - plasma * re, kerr * re - plasma * im))
        spectra = transform(groups_e + groups_n)
        c = coupling[...]
        for n in range(2):
            at = plane_of(2 * p + n)
            e_re, e_im = spectra[n]
            n_re, n_im = spectra[2 + n]
            fe[where, 0, at, :] = e_re
            fe[where, 1, at, :] = e_im
            part[where - 2, 0, at, :] = e_re - c * n_im
            part[where - 2, 1, at, :] = e_im + c * n_re

    def halo_four(slot, where, p):
        spectra = transform([series(slot, 4 * p + y) for y in range(4)])
        for y in range(4):
            at = plane_of(4 * p + y)
            side[where, 0, at, :], side[where, 1, at, :] = spectra[y]

    def swap(i):
        where = 4 + i - 2 * odd
        return pltpu.make_async_remote_copy(
            src_ref=fe.at[where],
            dst_ref=fe.at[jnp.where(odd == 0, i, 6 + i)],
            send_sem=swap_send.at[i],
            recv_sem=swap_recv.at[i],
            device_id=(me + 1 - 2 * odd, g),
            device_id_type=MESH,
        )

    def spectrum_to_partner(n):
        return pltpu.make_async_remote_copy(
            src_ref=fe.at[jnp.where(odd == 0, 2 + n, 5 - n)],
            dst_ref=halo_out.at[n],
            send_sem=halo_send.at[n],
            recv_sem=halo_recv.at[n],
            device_id=(partner, partner_gx),
            device_id_type=MESH,
        )

    start = jnp.where(at_end, 0, BOUNDARY_STEP)

    def own_row(step, carry):
        @pl.when(jnp.logical_and(step == start, plain))
        def _():
            share(lambda rows: wait_for(recv_sem.at[AHEAD], 2, rows), of_partner=True)

        @pl.when(jnp.logical_and(step == start, at_end))
        def _():
            wait_for(recv_sem.at[OWN], 2, 1024)

        boundary = jnp.logical_and(step >= start, step < start + 2)
        i = jnp.where(boundary, step - start, jnp.where(step < start, step, step - 2))
        for n in range(2):

            @pl.when(jnp.logical_and(jnp.logical_not(boundary), i == n))
            def _(n=n):
                wait_for(recv_sem.at[INNER + n], 1, 1024)

        @pl.when(jnp.logical_and(step == FORWARD_STEP - 1, plain))
        def _():
            forward_halo()

        near_first = jnp.where(odd == 0, 2 + i, 1 - i)
        slot = jnp.where(boundary, near_first, 4 + i)
        where = jnp.where(boundary, near_first + 4 * odd, 4 + i - 2 * odd)

        def body(p, carry):
            own_pair(slot, where, p)
            return carry

        lax.fori_loop(0, Y // 2, body, 0, unroll=4)
        for n in range(2):

            @pl.when(jnp.logical_and(jnp.logical_not(boundary), i == n))
            def _(n=n):
                swap(n).start()

            @pl.when(jnp.logical_and(spectral, step == n))
            def _(n=n):
                spectrum_to_partner(n).start()

        return carry

    lax.fori_loop(0, ROWS, own_row, 0)

    def inner_terms(row):
        def block(n, carry):
            k = pl.multiple_of(n * 8, 8)
            d = diffraction[pl.ds(k, 8), :] * (1.0 / 12.0)
            lap = []
            for c in range(2):
                mid = [fe[row + 2, c, pl.ds(y * R + k, 8), :] for y in range(Y)]
                planes = []
                for y in range(Y):
                    at = pl.ds(y * R + k, 8)
                    near = fe[row + 1, c, at, :] + fe[row + 3, c, at, :]
                    far = fe[row, c, at, :] + fe[row + 4, c, at, :]
                    for o in (-1, 1):
                        if 0 <= y + o < Y:
                            near = near + mid[y + o]
                    for o in (-2, 2):
                        if 0 <= y + o < Y:
                            far = far + mid[y + o]
                    planes.append(16.0 * near - far - 60.0 * mid[y])
                lap.append(planes)
            for y in range(Y):
                at = pl.ds(y * R + k, 8)
                to = pl.ds(k * Y + y, 8, stride=Y)
                result[row, 0, to, :] = part[row, 0, at, :] - d * lap[1][y]
                result[row, 1, to, :] = part[row, 1, at, :] + d * lap[0][y]
            return carry

        lax.fori_loop(0, R // 8, block, 0)
        pltpu.make_async_copy(result.at[row], q_out.at[:, row], out_sem.at[row]).start()

    def terms_step(step, carry):
        @pl.when(step == 2)
        def _():
            for n in range(2):
                swap(n).wait_recv()

        inner_terms(jnp.where(odd == 0, step, ROWS - 1 - step))
        return carry

    lax.fori_loop(0, ROWS, terms_step, 0)

    def halo_step(n, carry):
        for i, kind in enumerate((NEAR, FAR)):

            @pl.when(n == i)
            def _(kind=kind):
                share(lambda rows: wait_for(recv_sem.at[kind], 1, rows), of_partner=True)

        slot = jnp.where(odd == 0, 1 - n, 2 + n)

        def body(p, carry):
            halo_four(slot, n, p)
            return carry

        lax.fori_loop(0, Y // 4, body, 0, unroll=2)
        side_copy(n).start()
        return carry

    @pl.when(plain)
    def _():
        lax.fori_loop(0, 2, halo_step, 0)

    for row in range(ROWS):
        pltpu.make_async_copy(result.at[row], q_out.at[:, row], out_sem.at[row]).wait()
    for n in range(2):
        swap(n).wait_send()
        wait_for(send_sem.at[INNER + n], 1, 31 * 32)
    wait_for(send_sem.at[OWN], 2, 19 * 32)

    @pl.when(plain)
    def _():
        wait_for(send_sem.at[THEIRS], 2, 11 * 32)
        share(lambda rows: wait_for(send_sem.at[AHEAD], 2, rows))
        share(lambda rows: wait_for(send_sem.at[NEAR], 1, rows))
        share(lambda rows: wait_for(send_sem.at[FAR], 1, rows))

    @pl.when(at_end)
    def _():
        wait_for(send_sem.at[THEIRS], 2, 12 * 32)

    @pl.when(spectral)
    def _():
        for n in range(2):
            spectrum_to_partner(n).wait()

    @pl.when(jnp.logical_or(plain, tip))
    def _():
        for n in range(2):
            side_copy(n).wait()


def add_halo(
    q_in, halo_in, diffraction_in, out,
    q, halo, diffraction, result, staged, q_sem, halo_sem, d_sem, out_sem, copy_sem,
):
    odd = lax.rem(lax.axis_index("ta"), 2)
    base = 2 * odd
    depth = R // PIECES

    def copies(n):
        wide = pl.ds(n * depth * Y, depth * Y)
        thin = pl.ds(n * depth, depth)
        rows = pl.ds(base, 2)
        return (
            pltpu.make_async_copy(q_in.at[:, rows, wide], q.at[:, :, wide], q_sem.at[n]),
            pltpu.make_async_copy(
                halo_in.at[:, :, :, thin], halo.at[:, :, :, thin], halo_sem.at[n]
            ),
            pltpu.make_async_copy(result.at[:, :, wide], out.at[:, rows, wide], out_sem.at[n]),
        )

    first = pltpu.make_async_copy(diffraction_in, diffraction, d_sem)
    first.start()
    others = pl.ds(2 - base, 2)
    same_in = pltpu.make_async_copy(q_in.at[:, others], staged, copy_sem.at[0])
    same_out = pltpu.make_async_copy(staged, out.at[:, others], copy_sem.at[1])
    for n in range(PIECES):
        for copy in copies(n)[:2]:
            copy.start()
        if n == COPY_AFTER:
            same_in.start()
    first.wait()
    for n in range(PIECES):
        for copy in copies(n)[:2]:
            copy.wait()

        def block(i, carry, n=n):
            k = pl.multiple_of(n * depth + 8 * i, 8)
            at_k = pl.ds(k, 8)
            d = diffraction[at_k, :] * (1.0 / 12.0)
            for y in range(Y):
                outer, second = [], []
                for c in range(2):
                    near, far = halo[0, c, y, at_k, :], halo[1, c, y, at_k, :]
                    outer.append(16.0 * near - far)
                    second.append(-near)
                at = pl.ds(k * Y + y, 8, stride=Y)
                for row, lap in ((odd, outer), (1 - odd, second)):
                    result[0, row, at, :] = q[0, row, at, :] - d * lap[1]
                    result[1, row, at, :] = q[1, row, at, :] + d * lap[0]
            return carry

        lax.fori_loop(0, depth // 8, block, 0)
        copies(n)[2].start()
        if n == COPY_AFTER:
            same_in.wait()
            same_out.start()
    same_out.wait()
    for n in range(PIECES):
        copies(n)[2].wait()


def on_device(field, ion_rate, diffraction, coupling):
    x_rows = field.shape[1]
    tiles = field.reshape(2, x_rows, Y, 4, R).transpose(0, 1, 3, 2, 4).reshape(2, x_rows, 32, R)
    dft, twist, within, before = tables()
    hbm = pl.BlockSpec(memory_space=pl.ANY)
    q, halo = pl.pallas_call(
        kernel,
        out_shape=[
            jax.ShapeDtypeStruct((2, ROWS, R * Y, R), F32),
            jax.ShapeDtypeStruct((2, 2, Y * R, R), F32),
        ],
        in_specs=[hbm] * 8,
        out_specs=[hbm, hbm],
        scratch_shapes=[
            pltpu.VMEM((2, ROWS + 2, R * Y, R), F32),
            pltpu.VMEM((ROWS + 4, 2, Y * R, R), F32),
            pltpu.VMEM((ROWS, 2, Y * R, R), F32),
            pltpu.VMEM((ROWS, 2, R * Y, R), F32),
            pltpu.VMEM((2, 2, Y * R, R), F32),
            pltpu.SMEM((Y, x_rows), F32),
            pltpu.VMEM((R, R), F32),
            pltpu.VMEM((R, R), F32),
            pltpu.VMEM(dft.shape, BF16),
            pltpu.VMEM(twist.shape, F32),
            pltpu.VMEM(within.shape, BF16),
            pltpu.VMEM(before.shape, BF16),
            pltpu.SemaphoreType.DMA((7,)),
            pltpu.SemaphoreType.DMA((7,)),
            pltpu.SemaphoreType.DMA((7,)),
            pltpu.SemaphoreType.DMA((2,)),
            pltpu.SemaphoreType.DMA((2,)),
            pltpu.SemaphoreType.DMA((2,)),
            pltpu.SemaphoreType.DMA((2,)),
            pltpu.SemaphoreType.DMA((2,)),
            pltpu.SemaphoreType.DMA((ROWS,)),
        ],
        compiler_params=pltpu.CompilerParams(
            collective_id=0, has_side_effects=True, vmem_limit_bytes=60 * 1024 * 1024
        ),
    )(
        ion_rate.T,
        tiles,
        coupling.reshape(R, R),
        diffraction.reshape(R, R),
        jnp.asarray(dft),
        jnp.asarray(twist),
        jnp.asarray(within),
        jnp.asarray(before),
    )
    spectrum = pl.pallas_call(
        add_halo,
        out_shape=jax.ShapeDtypeStruct((2, ROWS, R * Y, R), F32),
        in_specs=[hbm] * 3,
        out_specs=hbm,
        scratch_shapes=[
            pltpu.VMEM((2, 2, R * Y, R), F32),
            pltpu.VMEM((2, 2, Y, R, R), F32),
            pltpu.VMEM((R, R), F32),
            pltpu.VMEM((2, 2, R * Y, R), F32),
            pltpu.VMEM((2, 2, R * Y, R), F32),
            pltpu.SemaphoreType.DMA((PIECES,)),
            pltpu.SemaphoreType.DMA((PIECES,)),
            pltpu.SemaphoreType.DMA,
            pltpu.SemaphoreType.DMA((PIECES,)),
            pltpu.SemaphoreType.DMA((2,)),
        ],
        compiler_params=pltpu.CompilerParams(vmem_limit_bytes=60 * 1024 * 1024),
    )(q, halo.reshape(2, 2, Y, R, R), diffraction.reshape(R, R))
    spectrum = spectrum.reshape(2, ROWS, R, Y, R).transpose(0, 1, 3, 2, 4)
    return spectrum.reshape(2, ROWS, Y, R * R)


def solution(mesh):
    in_specs = (P(None, "gx", None, "ta"), P("gx", None), P(), P())
    out_specs = P(None, ("gx", "ta"), None, None)
    return jax.shard_map(
        on_device, mesh=mesh, in_specs=in_specs, out_specs=out_specs, check_vma=False
    )
```
